1024 devices in a mesh: lon: 64 (over x_lo, z), hid: 16 (over x_hi, y, core).
Axes of the slice: x: 4 (x_hi: 2, x_lo: 2; x = x_hi * 2 + x_lo), y: 4, z: 32, core: 2. Of those that a mesh axis runs over, the one named last changes fastest.
Arguments:
- observations: bfloat16 [2097152, 64], P('lon'), may hold values from -6 to 6
- block_owner: int32 [16384, 1], P('lon'), may hold values from 0 to 63; in each aligned block of 64 rows (0 to 63, 64 to 127, ...) at most 2 rows name the same one
- block_tile: int32 [16384], P('lon'), may hold values from 0 to 9
- embed_weight: bfloat16 [64, 512], P(None, 'hid'), may hold values from -0.75 to 0.75
- embed_bias: float32 [512], P('hid'), may hold values from -1.5 to 1.5
- mesh_latent: bfloat16 [81920, 512], P('lon', 'hid'), may hold values from -6 to 6
- norm_gain: float32 [512], replicated, may hold values from 0.5 to 1.5
- w_gate: bfloat16 [512, 512], P(None, 'hid'), may hold values from -0.25 to 0.25
- w_up: bfloat16 [512, 512], P(None, 'hid'), may hold values from -0.25 to 0.25
- w_down: bfloat16 [512, 512], P('hid'), may hold values from -0.25 to 0.25
Outputs:
- new_latent: bfloat16 [81920, 512], P('lon', 'hid')
The draws below stay inside these ranges and needn't reach their ends.
Inputs may be any that keep to these rules, and one draw needn't show every extreme that they name: `block_owner`: blocks of one device come in 4 aligned sub-windows of 64 blocks; within one sub-window at most 2 blocks name the same owner, a bound that some block reaches.
All inputs are finite; a program needn't handle non-finite values.
Results may differ from the reference program's by a relative error of at most 0.0055.
Values may be sent and summed in bfloat16 or wider, within the bound.
A program may use at most 64 MiB of HBM per device.

```python
import math
import jax
import jax.numpy as jnp
import numpy as np
from jax import lax

CH = 64
LAT = 512
FFN = 512
BLK = 128
CAP = 2
TILES_DEV = 10
SUB_BLK = 64
BLK_DEV = 256
NBLK = 16384
OBS = 2097152
NODES = 81920
N_LON = 64


def touch_ends(drawn, rng, least, high):
    longest = drawn.shape.index(max(drawn.shape))
    spots = []
    for shift in (0, 1):
        where = [jax.random.randint(jax.random.fold_in(rng, axis), (), 0, length) for axis, length in enumerate(drawn.shape)]
        where[longest] = (where[longest] + shift) % drawn.shape[longest]
        spots.append(tuple(where))
    return drawn.at[spots[0]].set(least).at[spots[1]].set(high)


def block_levels(stream_key, shape, cuts, smallest, top_value):
    def one(position, parts):
        draws = jax.random.uniform(jax.random.fold_in(jax.random.fold_in(stream_key, 6), position), (parts,), jnp.float32, smallest / len(cuts), top_value / len(cuts))
        return jnp.repeat(jnp.exp(draws), shape[position] // parts).reshape((-1,) + (1,) * (len(shape) - position - 1))

    gain = one(*cuts[0])
    for cut in cuts[1:]:
        gain = gain * one(*cut)
    return gain


def assign_block(own_key, own, number, rows, count, top, most, slope):
    ranking = jax.random.permutation(own_key, count)
    packed, usual = load_shares(count, rows * top, most, slope, True), load_shares(count, rows * top, most, slope, False)
    places = jnp.arange(count)

    def named(sizes, turn):
        used = int((sizes > 0).sum())
        fixed = max(1, used // 4)
        shifted = fixed + (places - fixed + turn * (used - fixed)) % max(1, count - fixed)
        return jnp.zeros((count,), jnp.int32).at[ranking[jnp.where(places < fixed, places, shifted)]].set(jnp.asarray(sizes, jnp.int32))

    sizes = jnp.where(number % 4 == 0, named(packed, number // 4), named(usual, number - number // 4 - 1))
    mixed = jax.random.permutation(jax.random.fold_in(own, 3), count)
    donor, sink = mixed[0:count // 2 * 2:2], mixed[1:count // 2 * 2:2]
    room = jnp.minimum(sizes[donor] - 1, most - sizes[sink]) // 2
    room = jnp.where((donor == ranking[0]) | (sink == ranking[0]) | (sizes[sink] == 0), 0, jnp.maximum(room, 0))
    shifted = jax.random.randint(jax.random.fold_in(own, 4), (count // 2,), 0, 1 << 20) % (room + 1)
    sizes = sizes.at[donor].add(-shifted).at[sink].add(shifted)
    labels = jnp.searchsorted(jnp.cumsum(sizes), jnp.arange(rows * top), side="right").astype(jnp.int32)
    table = labels.reshape(top, rows).T
    table = table[jax.random.permutation(jax.random.fold_in(own, 1), rows)]
    turn = jax.random.randint(jax.random.fold_in(own, 2), (rows, 1), 0, top)
    return jnp.take_along_axis(table, (jnp.arange(top)[None, :] + turn) % top, axis=1)


def load_shares(amount, total, most, skew, full):
    portions = [(1 << 20) // math.isqrt(rank ** skew) + 1 for rank in range(1, amount + 1)]
    largest = most if full else min(most, max(-(-total // amount), total * portions[0] // sum(portions)))
    least = 1 if total - largest >= amount - 1 else 0
    given, rest = [largest] + [least] * (amount - 1), total - largest - least * (amount - 1)
    while rest > 0:
        movable = [i for i in range(1, amount) if given[i] < largest] or [i for i in range(1, amount) if given[i] < most]
        mass, left = sum([portions[i] for i in movable]), rest
        for i in movable:
            more = min(most - given[i], max(1, left * portions[i] // mass), rest)
            given[i] = given[i] + more
            rest = rest - more
    return np.array(given)


def normal_values(key, extent, scale, limit, pieces=(), dtype=jnp.bfloat16):
    level = block_levels(key, extent, pieces, -0.22, 0.18) if pieces else 1.0
    array = jax.random.normal(key, extent, jnp.float32) * scale * level
    return jnp.minimum(jnp.maximum(array, -limit), limit).astype(dtype)


def setup_inputs(seed: int = 0) -> dict:
    keys = jax.random.split(jax.random.key(seed), 11)
    observations = normal_values(keys[0], (OBS, CH), 1.0, 6.0, ((0, 64),))
    block_owner_keys = jax.random.split(jax.random.fold_in(keys[1], 1), NBLK // SUB_BLK)
    block_owner_turns = jax.random.permutation(jax.random.fold_in(keys[1], 3), NBLK // SUB_BLK)
    block_owner = jax.vmap(lambda own, number: assign_block(jax.random.fold_in(keys[1], 2), own, number, SUB_BLK, N_LON, 1, CAP, 2))(block_owner_keys, block_owner_turns).reshape((NBLK, 1))
    block_tile = touch_ends(jax.random.randint(keys[2], (NBLK,), 0, TILES_DEV), jax.random.fold_in(keys[2], 1), 0, TILES_DEV - 1).astype(jnp.int32)
    embed_weight = normal_values(keys[3], (CH, LAT), CH ** -0.5, 0.75, ((1, 16),))
    embed_bias = normal_values(keys[4], (LAT,), 0.3, 1.5, ((0, 16),), jnp.float32)
    mesh_latent = normal_values(keys[5], (NODES, LAT), 1.0, 6.0, ((0, 64), (1, 16)))
    norm_gain = jnp.clip(jax.random.uniform(keys[6], (LAT,), jnp.float32, 0.5, 1.5), 0.5, 1.5)
    w_gate = normal_values(keys[7], (LAT, FFN), LAT ** -0.5, 0.25, ((1, 16),))
    w_up = normal_values(keys[8], (LAT, FFN), LAT ** -0.5, 0.25, ((1, 16),))
    w_down = normal_values(keys[9], (FFN, LAT), FFN ** -0.5, 0.25, ((0, 16),))
    return {"observations": observations, "block_owner": block_owner, "block_tile": block_tile, "embed_weight": embed_weight, "embed_bias": embed_bias, "mesh_latent": mesh_latent, "norm_gain": norm_gain, "w_gate": w_gate, "w_up": w_up, "w_down": w_down}


def reference(observations, block_owner, block_tile, embed_weight, embed_bias, mesh_latent, norm_gain, w_gate, w_up, w_down):
    tile_total = TILES_DEV * N_LON
    width = embed_weight.shape[1]
    target = (block_owner[:, 0] * TILES_DEV + block_tile).astype(jnp.int32)
    obs_groups = observations.reshape(N_LON, BLK_DEV * BLK, CH)
    target_groups = target.reshape(N_LON, BLK_DEV)

    def add_group(running, group):
        group_rows, group_targets = group
        embedded = (jnp.dot(group_rows, embed_weight, preferred_element_type=jnp.float32) + embed_bias).astype(jnp.bfloat16)
        embedded = embedded.reshape(BLK_DEV, BLK * width).astype(jnp.float32)
        return (running + jax.ops.segment_sum(embedded, group_targets, num_segments=tile_total), None)
    tile_sums, _ = lax.scan(add_group, jnp.zeros((tile_total, BLK * width), jnp.float32), (obs_groups, target_groups))
    smooth = tile_sums + 0.5 * (jnp.roll(tile_sums, 1, 0) + jnp.roll(tile_sums, -1, 0))
    agg_scale = math.sqrt(TILES_DEV / BLK_DEV)
    latent_f = mesh_latent.astype(jnp.float32)
    mixed = (latent_f + agg_scale * smooth.reshape(tile_total * BLK, width)).astype(jnp.bfloat16)
    mixed_f = lax.optimization_barrier(mixed).astype(jnp.float32)
    mean_square = lax.optimization_barrier(jnp.mean(mixed_f * mixed_f, axis=1, keepdims=True))
    normed = (mixed_f * lax.rsqrt(mean_square + 1e-05) * norm_gain).astype(jnp.bfloat16)
    gate_proj = jnp.dot(normed, w_gate, preferred_element_type=jnp.float32)
    up_proj = jnp.dot(normed, w_up, preferred_element_type=jnp.float32)
    hidden = (jax.nn.silu(gate_proj) * up_proj).astype(jnp.bfloat16)
    return (latent_f + jnp.dot(hidden, w_down, preferred_element_type=jnp.float32)).astype(jnp.bfloat16)
```

```python
import math

import jax
import jax.numpy as jnp
from jax import lax
from jax.sharding import PartitionSpec as P

BLK = 128
PAD = 16


def local(
    observations,
    block_owner,
    block_tile,
    embed_weight,
    embed_bias,
    mesh_latent,
    norm_gain,
    w_gate,
    w_up,
    w_down,
):
    lon = lax.axis_size("lon")
    hid = lax.axis_size("hid")
    h = lax.axis_index("hid")
    blocks = block_tile.shape[0]
    channels = observations.shape[1]
    tiles_dev = mesh_latent.shape[0] // BLK
    tiles = tiles_dev * lon
    part = channels // hid
    wg = lax.all_gather(w_gate, "hid", axis=1, tiled=True)
    wu = lax.all_gather(w_up, "hid", axis=1, tiled=True)
    wd = lax.all_gather(w_down, "hid", axis=0, tiled=True)
    we = lax.all_gather(embed_weight, "hid", axis=1, tiled=True)
    bias = lax.all_gather(embed_bias, "hid", axis=0, tiled=True)
    latent = lax.all_to_all(mesh_latent, "hid", split_axis=0, concat_axis=1, tiled=True)

    mine = lax.dynamic_slice_in_dim(observations.T, h * part, part, axis=0)
    data = mine.reshape(part, blocks, BLK).transpose(1, 0, 2).reshape(blocks, part * BLK)
    target = block_owner[:, 0] * tiles_dev + block_tile
    gap = lax.rem(jnp.arange(tiles, dtype=jnp.int32)[:, None] - target[None, :] + tiles, tiles)
    spread = jnp.where(gap == 0, 1.0, jnp.where((gap == 1) | (gap == tiles - 1), 0.5, 0.0))
    sums = jnp.dot(spread.astype(jnp.bfloat16), data, preferred_element_type=jnp.float32)
    counts = jnp.sum(spread, axis=1).reshape(lon, 1, tiles_dev)
    counts = jnp.pad(counts, ((0, 0), (0, PAD - 1 - tiles_dev), (0, part * BLK - tiles_dev)))
    sums = jnp.concatenate([sums.reshape(lon, tiles_dev, part * BLK), counts], axis=1)
    sums = lax.psum_scatter(sums.reshape(lon * PAD, part * BLK), "lon", scatter_dimension=0, tiled=True)
    n_tile = sums[tiles_dev, :tiles_dev]
    nodes = sums[:tiles_dev].reshape(tiles_dev, part, BLK).transpose(1, 0, 2).reshape(part, tiles_dev * BLK)
    nodes = lax.all_to_all(nodes, "hid", split_axis=1, concat_axis=0, tiled=True)
    share = nodes.shape[1]
    n_node = lax.dynamic_slice_in_dim(jnp.repeat(n_tile, BLK), h * share, share, axis=0)
    smooth = jnp.dot(nodes.T, we.astype(jnp.float32), precision=lax.Precision.HIGHEST) + n_node[:, None] * bias
    latent_f = latent.astype(jnp.float32)
    mixed = (latent_f + math.sqrt(tiles_dev / blocks) * smooth).astype(jnp.bfloat16).astype(jnp.float32)
    mean_square = jnp.mean(mixed * mixed, axis=1, keepdims=True)
    normed = (mixed * lax.rsqrt(mean_square + 1e-05) * norm_gain).astype(jnp.bfloat16)
    gate = jnp.dot(normed, wg, preferred_element_type=jnp.float32)
    up = jnp.dot(normed, wu, preferred_element_type=jnp.float32)
    hidden = (jax.nn.silu(gate) * up).astype(jnp.bfloat16)
    out = (latent_f + jnp.dot(hidden, wd, preferred_element_type=jnp.float32)).astype(jnp.bfloat16)
    return lax.all_to_all(out, "hid", split_axis=1, concat_axis=0, tiled=True)


def solution(mesh):
    return jax.shard_map(
        local,
        mesh=mesh,
        in_specs=(
            P("lon", None),
            P("lon", None),
            P("lon"),
            P(None, "hid"),
            P("hid"),
            P("lon", "hid"),
            P(),
            P(None, "hid"),
            P(None, "hid"),
            P("hid", None),
        ),
        out_specs=P("lon", "hid"),
        check_vma=False,
    )
```

```python
import functools
import math

import jax
import jax.numpy as jnp
from jax import lax
from jax.experimental import pallas as pl
from jax.experimental.pallas import tpu as pltpu
from jax.sharding import PartitionSpec as P

MESH = pl.DeviceIdType.MESH
BLK = 128
NX = 2
NZ = 32
NH = 16
LON = NX * NZ
QA = 4
KB = NZ // QA
TILES = 10
ROWS = 16
PART = 4
WIDE = 3 * BLK
PIECE = KB * ROWS
F32 = jnp.float32
BF16 = jnp.bfloat16


def kernel(
    scale,
    obs, owner, tile, weight, latent, gain, w_gate, w_up, w_down,
    out,
    slab, rows32, data, part, xin, mine, ain, summed, bin_, tiles_out, tiles_in, w_all, we_all, lat_all, gain_t, out_all,
    load_sem, own_sem, xs, xr, as_, ar, bs, br, ws, wr, es, er, ls, lr, ts, tr, os_, or_,
):
    lon = lax.axis_index("lon")
    h = lax.axis_index("hid")
    x = lon // NZ
    z = lax.rem(lon, NZ)
    off = 2 * lax.rem(h, 2)
    v = lax.rem(z + off, NZ)
    g = v // QA
    q = lax.rem(v, QA)

    def at_v(value):
        return (x * NZ + lax.rem(value - off + NZ, NZ), h)

    x_peer = (lax.rem(x + 1, NX) * NZ + z, h)
    a_peer = [at_v(g * QA + lax.rem(q + d, QA)) for d in range(QA)]
    b_peer = [at_v(lax.rem(g + d, KB) * QA + q) for d in range(KB)]
    h_index = [lax.rem(h + d, NH) for d in range(NH)]
    h_peer = [(lon, i) for i in h_index]

    barrier = pltpu.get_barrier_semaphore()
    peers = [x_peer] + a_peer[1:] + b_peer[1:] + h_peer[1:]
    for peer in peers:
        pl.semaphore_signal(barrier, inc=1, device_id=peer, device_id_type=MESH)

    load = pltpu.make_async_copy(obs.at[pl.ds(pl.multiple_of((h // 4) * 16, 16), 16)], slab, load_sem)
    load.start()
    share = w_down.shape[0]
    own = [
        pltpu.make_async_copy(w_gate, w_all.at[h, 0], own_sem.at[0]),
        pltpu.make_async_copy(w_up, w_all.at[h, 1], own_sem.at[1]),
        pltpu.make_async_copy(w_down, w_all.at[h, 2], own_sem.at[2]),
        pltpu.make_async_copy(weight, we_all.at[h], own_sem.at[3]),
    ]
    for copy in own:
        copy.start()
    gain_t[...] = jnp.broadcast_to(gain[...], (BLK, gain.shape[1])).T

    codes = []
    for step, weigh in ((0, 1.0), (-1, 0.5), (1, 0.5)):
        t = tile[...] + step
        o = owner[...]
        o = jnp.where(t < 0, (o + LON - 1) & (LON - 1), jnp.where(t >= TILES, (o + 1) & (LON - 1), o))
        t = jnp.where(t < 0, TILES - 1, jnp.where(t >= TILES, 0, t))
        u = ((o & (NZ - 1)) + off) & (NZ - 1)
        row = ((o >> 5) * NZ + (u & (QA - 1)) * KB + (u >> 2)) * ROWS + t
        codes.append((weigh, row, jnp.where(t < 6, row + 10, -1), jnp.where(t >= 6, row + 4, -1)))

    load.wait()

    half = 4096

    def widen(i, _):
        span = pl.ds(pl.multiple_of(i * half, half), half)
        rows32[:, span] = slab[:, span].astype(F32)
        return 0

    lax.fori_loop(0, slab.shape[1] // half, widen, 0)
    first = 4 * lax.rem(h, 4)
    blocks = data.shape[1]
    for c in range(PART):
        data[c] = rows32[pl.ds(first + c, 1), :].reshape(blocks, BLK).astype(BF16)

    chunk = 128
    ones = jnp.ones((blocks, BLK), BF16)

    def local_sums(m, _):
        base = pl.multiple_of(m * chunk, chunk)
        at = lax.broadcasted_iota(jnp.int32, (chunk, blocks), 0) + base

        def spread(which):
            total = jnp.zeros((chunk, blocks), F32)
            for code in codes:
                total = total + jnp.where(at == code[which], code[0], 0.0)
            return total.astype(BF16)

        def dot(a, b):
            return jnp.dot(a, b, preferred_element_type=F32)

        main = spread(1)
        counts = dot(main, ones).reshape(chunk // ROWS, ROWS, BLK)
        r = lax.broadcasted_iota(jnp.int32, counts.shape, 1)
        lane = lax.broadcasted_iota(jnp.int32, counts.shape, 2)
        counts = jnp.sum(jnp.where(r == lane, counts, 0.0), axis=1, keepdims=True)
        counts = jnp.where(r == TILES, counts, 0.0).reshape(chunk, BLK)
        span = pl.ds(base, chunk)
        part[span, 0:BLK] = (dot(main, data[0]) + dot(spread(2), data[3])).astype(BF16)
        part[span, BLK:2 * BLK] = (dot(main, data[1]) + dot(spread(3), data[3])).astype(BF16)
        part[span, 2 * BLK:] = (dot(main, data[2]) + counts).astype(BF16)
        return 0

    lax.fori_loop(0, LON * ROWS // chunk, local_sums, 0)
    for copy in own:
        copy.wait()

    pl.semaphore_wait(barrier, len(peers))

    def remote(src, dst, ss, rs, peer):
        return pltpu.make_async_remote_copy(
            src_ref=src, dst_ref=dst, send_sem=ss, recv_sem=rs, device_id=peer, device_id_type=MESH
        )

    order = [1, 2, 3, 0]
    other = lax.rem(x + 1, NX)

    def piece(side, d):
        return pl.ds(pl.multiple_of((side * QA + lax.rem(q + d, QA)) * PIECE, PIECE), PIECE)

    x_copies = {}
    for d in order:
        x_copies[d] = remote(part.at[piece(other, d)], xin.at[d], xs.at[d], xr.at[d], x_peer)
        x_copies[d].start()
    a_copies = {}
    for d in order:
        x_copies[d].wait_recv()
        total = part[piece(x, d), :].astype(F32) + xin[d].astype(F32)
        mine[d] = total.astype(BF16)
        if d:
            a_copies[d] = remote(mine.at[d], ain.at[d], as_.at[d], ar.at[d], a_peer[d])
            a_copies[d].start()

    w_copies = []
    for d in range(1, NH):
        to = h_index[d]
        lane = pl.ds(pl.multiple_of(lax.rem(to, TILES) * BLK, BLK), BLK)
        w_copies.append((
            remote(latent.at[:, lane], lat_all.at[h], ls.at[d], lr.at[d], h_peer[d]),
            remote(we_all.at[h], we_all.at[h], es.at[d], er.at[d], h_peer[d]),
            remote(w_all.at[h], w_all.at[h], ws.at[d], wr.at[d], h_peer[d]),
        ))

        @pl.when(to < TILES)
        def _():
            for copy in w_copies[d - 1]:
                copy.start()

    for d in range(1, QA):
        a_copies[d].wait_recv()
    for k in range(KB):
        at = pl.ds(k * ROWS, ROWS)
        total = mine[0, at].astype(F32)
        for d in range(1, QA):
            total = total + ain[d, at].astype(F32)
        summed[at] = total.astype(BF16)
    b_copies = {}
    for d in (4, 3, 5, 2, 6, 1, 7):
        at = pl.ds(pl.multiple_of(lax.rem(g + d, KB) * ROWS, ROWS), ROWS)
        b_copies[d] = remote(summed.at[at], bin_.at[d], bs.at[d], br.at[d], b_peer[d])
        b_copies[d].start()

    @pl.when(h < TILES)
    def _():
        lane = pl.ds(pl.multiple_of(lax.rem(h, TILES) * BLK, BLK), BLK)
        copy = pltpu.make_async_copy(latent.at[:, lane], lat_all.at[h], load_sem)
        copy.start()
        copy.wait()
        for d in range(1, NH):
            for copy in w_copies[d - 1]:
                copy.wait_recv()

    total = summed[pl.ds(pl.multiple_of(g * ROWS, ROWS), ROWS)].astype(F32)
    for d in range(1, KB):
        b_copies[d].wait_recv()
        total = total + bin_[d].astype(F32)

    tiles_out[...] = jnp.zeros(tiles_out.shape, F32)
    for i in range(TILES):
        for c in range(3):
            tiles_out[i, c:c + 1] = total[i:i + 1, c * BLK:(c + 1) * BLK]
        r, c = (10 + i, 0) if i < 6 else (4 + i, 1)
        tiles_out[i, 3:4] = total[r:r + 1, c * BLK:(c + 1) * BLK]
        tiles_out[i, 4:5] = jnp.broadcast_to(total[10:11, 2 * BLK + i:2 * BLK + i + 1], (1, BLK))
    t_copies = []
    for d in range(1, NH):
        to = h_index[d]
        t_copies.append(remote(tiles_out.at[lax.rem(to, TILES)], tiles_in.at[h], ts.at[d], tr.at[d], h_peer[d]))

        @pl.when(to < TILES)
        def _():
            t_copies[d - 1].start()

    o_copies = []
    me_lane = pl.ds(pl.multiple_of(lax.rem(h, TILES) * BLK, BLK), BLK)
    for d in range(1, NH):
        to = h_index[d]
        src = out_all.at[pl.ds(pl.multiple_of(to * share, share), share)]
        o_copies.append(remote(src, out.at[:, me_lane], os_.at[d], or_.at[d], h_peer[d]))

    @pl.when(h < TILES)
    def _():
        tiles_in[h] = tiles_out[lax.rem(h, TILES)]
        for copy in t_copies:
            copy.wait_recv()
        sums = tiles_in[...]
        number = sums[0, 4:5]
        sums = sums[:, 0:PART].reshape(NH * PART, BLK)
        extra = jnp.where(lax.broadcasted_iota(jnp.int32, (BLK - NH * PART, BLK), 0) < 3, number, 0.0)
        sums = jnp.concatenate([sums, extra], axis=0)
        we = we_all[...].reshape(NH * share, BLK)
        smooth = jnp.zeros((NH * share, BLK), F32)
        for _ in range(3):
            piece16 = sums.astype(BF16)
            smooth = smooth + jnp.dot(we, piece16, preferred_element_type=F32)
            sums = sums - piece16.astype(F32)
        lat = lat_all[...].reshape(NH * share, BLK).astype(F32)
        mixed = (lat + scale * smooth).astype(BF16).astype(F32)
        mean_square = jnp.mean(mixed * mixed, axis=0, keepdims=True)
        normed = (mixed * lax.rsqrt(mean_square + 1e-05) * gain_t[...]).astype(BF16)
        wide = w_gate.shape[1]
        gate = jnp.dot(w_all[:, 0].reshape(NH * share, wide), normed, preferred_element_type=F32)
        up = jnp.dot(w_all[:, 1].reshape(NH * share, wide), normed, preferred_element_type=F32)
        hidden = (gate / (1.0 + jnp.exp(-gate)) * up).astype(BF16)
        down = w_all[:, 2].reshape(NH * share, wide)
        value = lax.dot_general(down, hidden, (((0,), (0,)), ((), ())), preferred_element_type=F32)
        out_all[...] = (lat + value).astype(BF16)
        for copy in o_copies:
            copy.start()
        out[:, me_lane] = out_all[pl.ds(pl.multiple_of(h * share, share), share)]

    for d in range(1, NH):
        source = lax.rem(h + NH - d, NH)

        @pl.when(source < TILES)
        def _():
            o_copies[d - 1].wait_recv()

    for d in range(QA):
        x_copies[d].wait_send()
    for d in range(1, QA):
        a_copies[d].wait_send()
    for d in range(1, KB):
        b_copies[d].wait_send()
    for d in range(1, NH):

        @pl.when(h_index[d] < TILES)
        def _():
            for copy in w_copies[d - 1]:
                copy.wait_send()
            t_copies[d - 1].wait_send()

    @pl.when(h < TILES)
    def _():
        for copy in o_copies:
            copy.wait_send()


def local(observations, block_owner, block_tile, embed_weight, embed_bias, mesh_latent, norm_gain, w_gate, w_up, w_down):
    blocks = block_tile.shape[0]
    rows = observations.shape[0]
    share = embed_weight.shape[1]
    nodes = mesh_latent.shape[0]
    lat = norm_gain.shape[0]
    pieces, rest = [], embed_bias
    for _ in range(3):
        pieces.append(rest.astype(BF16))
        rest = rest - pieces[-1].astype(F32)
    spare = jnp.zeros((share, BLK - embed_weight.shape[0] - 3), BF16)
    weight = jnp.concatenate([embed_weight.T] + [p[:, None] for p in pieces] + [spare], axis=1)
    vmem = pl.BlockSpec(memory_space=pltpu.VMEM)
    anywhere = pl.BlockSpec(memory_space=pl.ANY)
    dma = pltpu.SemaphoreType.DMA
    out = pl.pallas_call(
        functools.partial(kernel, math.sqrt(TILES / blocks)),
        out_shape=jax.ShapeDtypeStruct((share, nodes), BF16),
        in_specs=[anywhere, vmem, vmem, vmem, vmem, vmem, anywhere, anywhere, anywhere],
        out_specs=vmem,
        scratch_shapes=[
            pltpu.VMEM((16, rows), BF16),
            pltpu.VMEM((16, rows), F32),
            pltpu.VMEM((PART, blocks, BLK), BF16),
            pltpu.VMEM((LON * ROWS, WIDE), BF16),
            pltpu.VMEM((QA, PIECE, WIDE), BF16),
            pltpu.VMEM((QA, PIECE, WIDE), BF16),
            pltpu.VMEM((QA, PIECE, WIDE), BF16),
            pltpu.VMEM((PIECE, WIDE), BF16),
            pltpu.VMEM((KB, ROWS, WIDE), BF16),
            pltpu.VMEM((TILES, 8, BLK), F32),
            pltpu.VMEM((NH, 8, BLK), F32),
            pltpu.VMEM((NH, 3, share, lat), BF16),
            pltpu.VMEM((NH, share, BLK), BF16),
            pltpu.VMEM((NH, share, BLK), BF16),
            pltpu.VMEM((lat, BLK), F32),
            pltpu.VMEM((lat, BLK), BF16),
            dma, dma((4,)),
            dma((QA,)), dma((QA,)), dma((QA,)), dma((QA,)), dma((KB,)), dma((KB,)),
            dma((NH,)), dma((NH,)), dma((NH,)), dma((NH,)), dma((NH,)), dma((NH,)),
            dma((NH,)), dma((NH,)), dma((NH,)), dma((NH,)),
        ],
        compiler_params=pltpu.CompilerParams(collective_id=0, has_side_effects=True, vmem_limit_bytes=40 * 2**20),
    )(
        observations.T, block_owner.T, block_tile[None, :], weight, mesh_latent.T, norm_gain[None, :],
        w_gate.T, w_up.T, w_down,
    )
    return out.T


def solution(mesh):
    return jax.shard_map(
        local,
        mesh=mesh,
        in_specs=(
            P("lon", None),
            P("lon", None),
            P("lon"),
            P(None, "hid"),
            P("hid"),
            P("lon", "hid"),
            P(),
            P(None, "hid"),
            P(None, "hid"),
            P("hid", None),
        ),
        out_specs=P("lon", "hid"),
        check_vma=False,
    )
```

```python
import functools
import math

import jax
import jax.numpy as jnp
from jax import lax
from jax.experimental import pallas as pl
from jax.experimental.pallas import tpu as pltpu
from jax.sharding import PartitionSpec as P

MESH = pl.DeviceIdType.MESH
BLK = 128
NX = 2
NZ = 32
NH = 16
NY = 4
LON = NX * NZ
QA = 4
KB = NZ // QA
TILES = 10
ROWS = 16
PART = 4
WIDE = 3 * BLK
PIECE = KB * ROWS
SPOTS = (4, 3, 5, 2, 6, 1, 7, 0)
F32 = jnp.float32
BF16 = jnp.bfloat16


def kernel(
    scale,
    obs, owner_in, tile_in, weight, bias_in, latent, gain_in, w_gate, w_up, w_down,
    out,
    owner, tile, bias, gain, we_own, slab, rows32, data, part, xin, mine, ain, summed, bin_,
    tiles_out, tiles_in, w_all, down_t, we_all, lat_all, gain_t, out_all,
    load_sem, own_sem, xs, xr, as_, ar, bs, br, wys, wyr, wxs, wxr, es, er, ls, lr, ts, tr, os_, or_,
):
    lon = lax.axis_index("lon")
    h = lax.axis_index("hid")
    x = lon // NZ
    z = lax.rem(lon, NZ)
    core = lax.rem(h, 2)
    y = lax.rem(h // 2, NY)
    xh = h // (2 * NY)
    off = 2 * core
    v = lax.rem(z + off, NZ)
    g = v // QA
    q = lax.rem(v, QA)

    def at_v(value):
        return (x * NZ + lax.rem(value - off + NZ, NZ), h)

    def at_hid(xh, y, core):
        return (lon, (xh * NY + y) * 2 + core)

    def active(to):
        return (lax.rem(to, 2) == 0) | (lax.rem(to // 2, NY) == 0)

    def tile_of(to):
        return (to // (2 * NY)) * (NY + 1) + jnp.where(lax.rem(to, 2) == 0, lax.rem(to // 2, NY), NY)

    x_peer = (lax.rem(x + 1, NX) * NZ + z, h)
    a_peer = [at_v(g * QA + lax.rem(q + d, QA)) for d in range(QA)]
    b_peer = [at_v(lax.rem(g + d, KB) * QA + q) for d in range(KB)]
    h_index = [lax.rem(h + d, NH) for d in range(NH)]
    h_peer = [(lon, i) for i in h_index]

    barrier = pltpu.get_barrier_semaphore()
    peers = [x_peer] + a_peer[1:] + b_peer[1:] + h_peer[1:]
    for peer in peers:
        pl.semaphore_signal(barrier, inc=1, device_id=peer, device_id_type=MESH)

    load = pltpu.make_async_copy(obs.at[pl.ds(pl.multiple_of((h // 4) * 16, 16), 16)], slab, load_sem)
    load.start()
    share = w_down.shape[0]
    place = core * (2 * NY) + xh * NY + y
    own = [
        pltpu.make_async_copy(owner_in, owner, own_sem.at[0]),
        pltpu.make_async_copy(tile_in, tile, own_sem.at[1]),
        pltpu.make_async_copy(w_gate, w_all.at[place, 0], own_sem.at[2]),
        pltpu.make_async_copy(w_up, w_all.at[place, 1], own_sem.at[3]),
        pltpu.make_async_copy(w_down, w_all.at[place, 2], own_sem.at[4]),
        pltpu.make_async_copy(bias_in, bias, own_sem.at[5]),
        pltpu.make_async_copy(gain_in, gain, own_sem.at[6]),
        pltpu.make_async_copy(weight, we_own, own_sem.at[7]),
    ]
    for copy in own:
        copy.start()
    own[0].wait()
    own[1].wait()

    codes = []
    for step, weigh in ((0, 1.0), (-1, 0.5), (1, 0.5)):
        t = tile[...] + step
        o = owner[...]
        o = jnp.where(t < 0, (o + LON - 1) & (LON - 1), jnp.where(t >= TILES, (o + 1) & (LON - 1), o))
        t = jnp.where(t < 0, TILES - 1, jnp.where(t >= TILES, 0, t))
        u = ((o & (NZ - 1)) + off) & (NZ - 1)
        side = (o >> 5) ^ x
        dq = ((u & (QA - 1)) - q) & (QA - 1)
        m = (((u >> 2) - g) & (KB - 1)) - KB // 2
        spot = jnp.where(m < 0, -2 * m - 1, 2 * m)
        codes.append((weigh, ((side * QA + dq) * KB + spot) * ROWS + t))

    blocks = data.shape[0]
    load.wait()

    def widen(b, _):
        rows = pl.ds(pl.multiple_of(b * 16, 16), 16)
        rows32[rows] = slab[:, pl.ds(pl.multiple_of(b * BLK, BLK), BLK)].astype(F32)
        return 0

    lax.fori_loop(0, blocks, widen, 0, unroll=16)
    first = PART * lax.rem(h, 4)
    for c in range(PART):
        data[:, c * BLK:(c + 1) * BLK] = rows32[pl.ds(first + c, blocks, stride=16), :].astype(BF16)
    data[:, PART * BLK:] = jnp.ones((blocks, BLK), BF16)

    def sums_of(side, d):
        at = lax.broadcasted_iota(jnp.int32, (PIECE, blocks), 0) + (side * QA + d) * PIECE
        spread = jnp.zeros((PIECE, blocks), F32)
        for weigh, code in codes:
            spread = jnp.where(at == code, weigh, spread)
        full = jnp.dot(spread.astype(BF16), data[...], preferred_element_type=F32)
        fourth = full[:, 3 * BLK:4 * BLK]
        r = lax.rem(lax.broadcasted_iota(jnp.int32, (PIECE, BLK), 0), ROWS)
        lane = lax.broadcasted_iota(jnp.int32, (PIECE, BLK), 1)
        counts = jnp.where(r == lane, full[:, 4 * BLK:], 0.0).reshape(KB, ROWS, BLK)
        counts = jnp.broadcast_to(jnp.sum(counts, axis=1, keepdims=True), (KB, ROWS, BLK)).reshape(PIECE, BLK)
        return [
            jnp.where(r < TILES, full[:, 0:BLK], pltpu.roll(fourth, 10, 0)),
            jnp.where(r < TILES, full[:, BLK:2 * BLK], pltpu.roll(fourth, 4, 0)),
            jnp.where(r < TILES, full[:, 2 * BLK:3 * BLK], counts),
        ]

    order = [1, 2, 3, 0]
    for d in order:
        for c, value in enumerate(sums_of(1, d)):
            part[d, :, c * BLK:(c + 1) * BLK] = value.astype(BF16)

    def remote(src, dst, ss, rs, peer):
        return pltpu.make_async_remote_copy(
            src_ref=src, dst_ref=dst, send_sem=ss, recv_sem=rs, device_id=peer, device_id_type=MESH
        )

    pl.semaphore_wait(barrier, len(peers))
    x_copies = {}
    for d in order:
        x_copies[d] = remote(part.at[d], xin.at[d], xs.at[d], xr.at[d], x_peer)
        x_copies[d].start()
    for copy in own[2:]:
        copy.wait()
    wy_copies = []
    for d in range(1, NY):
        ref = w_all.at[place]
        wy_copies.append(remote(ref, ref, wys.at[d], wyr.at[d], at_hid(xh, lax.rem(y + d, NY), core)))
        wy_copies[-1].start()

    half = PIECE // 2
    a_copies = {}
    for d in order:
        values = sums_of(0, d)
        x_copies[d].wait_recv()
        for c, value in enumerate(values):
            lanes = slice(c * BLK, (c + 1) * BLK)
            mine[d, :, lanes] = (value + xin[d, :, lanes].astype(F32)).astype(BF16)
        if d:
            for i in range(2):
                at = pl.ds(i * half, half)
                a_copies[d, i] = remote(mine.at[d, at], ain.at[d, at], as_.at[d, i], ar.at[d, i], a_peer[d])
            a_copies[d, 0].start()
    for d in range(1, QA):
        a_copies[d, 1].start()

    r = lax.broadcasted_iota(jnp.int32, (share, BLK), 0)
    lane = lax.broadcasted_iota(jnp.int32, (share, BLK), 1)
    spare = jnp.zeros((share, BLK - share), F32)
    row = jnp.concatenate([jnp.broadcast_to(bias[...], (share, share)), spare], axis=1)
    rest = jnp.sum(jnp.where(r == lane, row, 0.0), axis=1, keepdims=True)
    channels = NH * PART
    we_wide = jnp.concatenate([we_own[...].astype(F32), jnp.zeros((share, BLK - channels), F32)], axis=1)
    for i in range(3):
        digit = rest.astype(BF16).astype(F32)
        we_wide = jnp.where(lane == channels + i, digit, we_wide)
        rest = rest - digit
    we_all[h] = we_wide.astype(BF16)

    for copy in wy_copies:
        copy.wait_recv()
    ref = w_all.at[pl.ds(core * (2 * NY) + xh * NY, NY)]
    wx_copy = remote(ref, ref, wxs.at[0], wxr.at[0], at_hid(1 - xh, y, core))
    wx_copy.start()

    small = []
    for d in range(1, NH):
        to = h_index[d]
        lanes = pl.ds(pl.multiple_of(tile_of(to) * BLK, BLK), BLK)
        small.append((
            remote(latent.at[:, lanes], lat_all.at[h], ls.at[d], lr.at[d], h_peer[d]),
            remote(we_all.at[h], we_all.at[h], es.at[d], er.at[d], h_peer[d]),
        ))

        @pl.when(active(to))
        def _():
            for copy in small[d - 1]:
                copy.start()

    b_copies = {}
    for i in range(2):
        for d in range(1, QA):
            a_copies[d, i].wait_recv()
        at = pl.ds(i * half, half)
        total = mine[0, at].astype(F32)
        for d in range(1, QA):
            total = total + ain[d, at].astype(F32)
        summed[at] = total.astype(BF16)
        for spot in range(i * KB // 2, (i + 1) * KB // 2):
            d = SPOTS[spot]
            if d:
                rows = pl.ds(spot * ROWS, ROWS)
                b_copies[d] = remote(summed.at[rows], bin_.at[d], bs.at[d], br.at[d], b_peer[d])
                b_copies[d].start()
    my_lanes = pl.ds(pl.multiple_of(tile_of(h) * BLK, BLK), BLK)
    wx_copy.wait_recv()
    ref = w_all.at[pl.ds(core * (2 * NY), 2 * NY)]
    wc_copy = remote(ref, ref, wxs.at[1], wxr.at[1], at_hid(xh, y, 1 - core))
    wc_copy.start()
    gain_t[...] = jnp.broadcast_to(gain[...], (BLK, gain.shape[1])).T

    @pl.when(active(h))
    def _():
        copy = pltpu.make_async_copy(latent.at[:, my_lanes], lat_all.at[h], load_sem)
        copy.start()
        copy.wait()
        for copies in small:
            for copy in copies:
                copy.wait_recv()

    wide = w_gate.shape[1]
    wc_copy.wait_recv()
    down_t[...] = w_all[:, 2].reshape(NH * share, wide).T
    total = summed[pl.ds((KB - 1) * ROWS, ROWS)].astype(F32)
    for d in (1, 7, 2, 6, 3, 5, 4):
        b_copies[d].wait_recv()
        total = total + bin_[d].astype(F32)
    for i in range(TILES):
        for c in range(3):
            tiles_out[i, c:c + 1] = total[i:i + 1, c * BLK:(c + 1) * BLK]
        r, c = (10 + i, 0) if i < 6 else (4 + i, 1)
        tiles_out[i, 3:4] = total[r:r + 1, c * BLK:(c + 1) * BLK]
        tiles_out[i, 4:8] = jnp.broadcast_to(total[10:11, 2 * BLK + i:2 * BLK + i + 1], (4, BLK))
    t_copies = []
    for d in range(1, NH):
        to = h_index[d]
        t_copies.append(remote(tiles_out.at[tile_of(to)], tiles_in.at[h], ts.at[d], tr.at[d], h_peer[d]))

        @pl.when(active(to))
        def _():
            t_copies[d - 1].start()

    o_copies = []
    for d in range(1, NH):
        to = h_index[d]
        src = out_all.at[pl.ds(pl.multiple_of(to * share, share), share)]
        o_copies.append(remote(src, out.at[:, my_lanes], os_.at[d], or_.at[d], h_peer[d]))

    @pl.when(active(h))
    def _():
        tiles_in[h] = tiles_out[tile_of(h)]
        for copy in t_copies:
            copy.wait_recv()
        sums = tiles_in[...]
        number = sums[0, 4:5]
        sums = sums[:, 0:PART].reshape(channels, BLK)
        extra = jnp.where(lax.broadcasted_iota(jnp.int32, (BLK - channels, BLK), 0) < 3, number, 0.0)
        sums = jnp.concatenate([sums, extra], axis=0)
        we = we_all[...].reshape(NH * share, BLK)
        smooth = jnp.zeros((NH * share, BLK), F32)
        for _ in range(3):
            digit = sums.astype(BF16)
            smooth = smooth + jnp.dot(we, digit, preferred_element_type=F32)
            sums = sums - digit.astype(F32)
        lat = lat_all[...].reshape(NH * share, BLK).astype(F32)
        mixed = (lat + scale * smooth).astype(BF16).astype(F32)
        mean_square = jnp.mean(mixed * mixed, axis=0, keepdims=True)
        normed = (mixed * lax.rsqrt(mean_square + 1e-05) * gain_t[...]).astype(BF16)
        gate = jnp.dot(w_all[:, 0].reshape(NH * share, wide), normed, preferred_element_type=F32)
        up = jnp.dot(w_all[:, 1].reshape(NH * share, wide), normed, preferred_element_type=F32)
        hidden = (gate / (1.0 + jnp.exp(-gate)) * up).astype(BF16)
        value = jnp.dot(down_t[...], hidden, preferred_element_type=F32)
        out_all[...] = (lat + value).astype(BF16)
        for copy in o_copies:
            copy.start()
        copy = pltpu.make_async_copy(
            out_all.at[pl.ds(pl.multiple_of(h * share, share), share)], out.at[:, my_lanes], load_sem
        )
        copy.start()
        copy.wait()

    for d in range(1, NH):

        @pl.when(active(lax.rem(h + NH - d, NH)))
        def _():
            o_copies[d - 1].wait_recv()

    sent = list(x_copies.values()) + list(a_copies.values()) + list(b_copies.values())
    for copy in sent + wy_copies + [wx_copy, wc_copy]:
        copy.wait_send()
    for d in range(1, NH):

        @pl.when(active(h_index[d]))
        def _():
            for copy in small[d - 1]:
                copy.wait_send()
            t_copies[d - 1].wait_send()

    @pl.when(active(h))
    def _():
        for copy in o_copies:
            copy.wait_send()


def local(observations, block_owner, block_tile, embed_weight, embed_bias, mesh_latent, norm_gain, w_gate, w_up, w_down):
    blocks = block_tile.shape[0]
    rows = observations.shape[0]
    share = embed_weight.shape[1]
    nodes = mesh_latent.shape[0]
    lat = norm_gain.shape[0]
    hbm = pl.BlockSpec(memory_space=pltpu.HBM)
    dma = pltpu.SemaphoreType.DMA
    out = pl.pallas_call(
        functools.partial(kernel, math.sqrt(TILES / blocks)),
        out_shape=jax.ShapeDtypeStruct((share, nodes), BF16),
        in_specs=[hbm] * 10,
        out_specs=hbm,
        scratch_shapes=[
            pltpu.VMEM((1, blocks), jnp.int32),
            pltpu.VMEM((1, blocks), jnp.int32),
            pltpu.VMEM((1, share), F32),
            pltpu.VMEM((1, lat), F32),
            pltpu.VMEM((share, NH * PART), BF16),
            pltpu.VMEM((16, rows), BF16),
            pltpu.VMEM((blocks * 16, BLK), F32),
            pltpu.VMEM((blocks, (PART + 1) * BLK), BF16),
            pltpu.VMEM((QA, PIECE, WIDE), BF16),
            pltpu.VMEM((QA, PIECE, WIDE), BF16),
            pltpu.VMEM((QA, PIECE, WIDE), BF16),
            pltpu.VMEM((QA, PIECE, WIDE), BF16),
            pltpu.VMEM((PIECE, WIDE), BF16),
            pltpu.VMEM((KB, ROWS, WIDE), BF16),
            pltpu.VMEM((TILES, 8, BLK), F32),
            pltpu.VMEM((NH, 8, BLK), F32),
            pltpu.VMEM((NH, 3, share, lat), BF16),
            pltpu.VMEM((lat, NH * share), BF16),
            pltpu.VMEM((NH, share, BLK), BF16),
            pltpu.VMEM((NH, share, BLK), BF16),
            pltpu.VMEM((lat, BLK), F32),
            pltpu.VMEM((lat, BLK), BF16),
            dma, dma((8,)),
            dma((QA,)), dma((QA,)), dma((QA, 2)), dma((QA, 2)), dma((KB,)), dma((KB,)),
            dma((NY,)), dma((NY,)), dma((2,)), dma((2,)),
            dma((NH,)), dma((NH,)), dma((NH,)), dma((NH,)), dma((NH,)), dma((NH,)), dma((NH,)), dma((NH,)),
        ],
        compiler_params=pltpu.CompilerParams(collective_id=0, has_side_effects=True, vmem_limit_bytes=64 * 2**20),
    )(
        observations.T, block_owner.T, block_tile[None, :], embed_weight.T, embed_bias[None, :], mesh_latent.T, norm_gain[None, :],
        w_gate.T, w_up.T, w_down,
    )
    return out.T


def solution(mesh):
    return jax.shard_map(
        local,
        mesh=mesh,
        in_specs=(
            P("lon", None),
            P("lon", None),
            P("lon"),
            P(None, "hid"),
            P("hid"),
            P("lon", "hid"),
            P(),
            P(None, "hid"),
            P(None, "hid"),
            P("hid", None),
        ),
        out_specs=P("lon", "hid"),
        check_vma=False,
    )
```

```python
import functools
import math

import jax
import jax.numpy as jnp
from jax import lax
from jax.experimental import pallas as pl
from jax.experimental.pallas import tpu as pltpu
from jax.sharding import PartitionSpec as P

MESH = pl.DeviceIdType.MESH
BLK = 128
NX = 2
NZ = 32
NH = 16
NY = 4
LON = NX * NZ
QA = 4
KB = NZ // QA
TILES = 10
ROWS = 16
PART = 8
NG = NH // 2
HALF = TILES // 2
WIDE = 3 * BLK
PIECE = KB * ROWS
PHASES = KB // 2
SPOTS = (2, 6, 1, 7, 3, 5, 4, 0)
NEAR = (1, 7, 2, 6)
F32 = jnp.float32
BF16 = jnp.bfloat16


def kernel(
    scale,
    obs, owner_in, tile_in, weight, bias_in, latent, gain_in, w_gate, w_up, w_down,
    out,
    owner, tile, bias, gain, we_own, slab, rows32, data, part, xin, mine, ain, summed, bin_,
    tiles_out, tiles_in, w_all, down_t, we_all, lat_all, gain_t, out_all,
    relay, load_sem, own_sem, xs, xr, as_, ar, bs, br, wys, wyr, wxs, wxr, es, er, ls, lr, ts, tr, os_, or_,
):
    lon = lax.axis_index("lon")
    h = lax.axis_index("hid")
    group = lax.rem(h, NG)
    x = lon // NZ
    z = lax.rem(lon, NZ)
    core = lax.rem(h, 2)
    y = lax.rem(h // 2, NY)
    xh = h // (2 * NY)
    off = 2 * core
    v = lax.rem(z + off, NZ)
    g = v // QA
    q = lax.rem(v, QA)

    def at_v(value):
        return (x * NZ + lax.rem(value - off + NZ, NZ), h)

    def at_hid(xh, y, core):
        return (lon, (xh * NY + y) * 2 + core)

    def active(to):
        return (lax.rem(to, 2) == 0) | (lax.rem(to // 2, NY) == 0)

    def tile_of(to):
        return (to // (2 * NY)) * (NY + 1) + jnp.where(lax.rem(to, 2) == 0, lax.rem(to // 2, NY), NY)

    x_peer = (lax.rem(x + 1, NX) * NZ + z, h)
    a_peer = [at_v(g * QA + lax.rem(q + d, QA)) for d in range(QA)]
    b_peer = [at_v(lax.rem(g + d, KB) * QA + q) for d in range(KB)]
    h_index = [lax.rem(h + d, NH) for d in range(NH)]
    h_peer = [(lon, i) for i in h_index]

    barrier = pltpu.get_barrier_semaphore()
    peers = [x_peer] + a_peer[1:] + [b_peer[d] for d in NEAR] + h_peer[1:]
    for peer in peers:
        pl.semaphore_signal(barrier, inc=1, device_id=peer, device_id_type=MESH)

    load = pltpu.make_async_copy(obs.at[pl.ds(pl.multiple_of((group // 2) * 16, 16), 16)], slab, load_sem)
    load.start()
    share = w_down.shape[0]
    place = core * (2 * NY) + xh * NY + y
    own = [
        pltpu.make_async_copy(owner_in, owner, own_sem.at[0]),
        pltpu.make_async_copy(tile_in, tile, own_sem.at[1]),
        pltpu.make_async_copy(w_gate, w_all.at[place, 0], own_sem.at[2]),
        pltpu.make_async_copy(w_up, w_all.at[place, 1], own_sem.at[3]),
        pltpu.make_async_copy(w_down, w_all.at[place, 2], own_sem.at[4]),
        pltpu.make_async_copy(bias_in, bias, own_sem.at[5]),
        pltpu.make_async_copy(gain_in, gain, own_sem.at[6]),
        pltpu.make_async_copy(weight, we_own, own_sem.at[7]),
    ]
    for copy in own:
        copy.start()
    own[0].wait()
    own[1].wait()

    codes = []
    for step, weigh in ((0, 1.0), (-1, 0.5), (1, 0.5)):
        t = tile[...] + step
        o = owner[...]
        o = jnp.where(t < 0, (o + LON - 1) & (LON - 1), jnp.where(t >= TILES, (o + 1) & (LON - 1), o))
        t = jnp.where(t < 0, TILES - 1, jnp.where(t >= TILES, 0, t))
        u = ((o & (NZ - 1)) + off) & (NZ - 1)
        side = (o >> 5) ^ x
        dq = ((u & (QA - 1)) - q) & (QA - 1)
        dk = ((u >> 2) - g) & (KB - 1)
        spot = jnp.full(dk.shape, KB - 1, jnp.int32)
        for place_of, d in enumerate(SPOTS[:-1]):
            spot = jnp.where(dk == d, place_of, spot)
        t = t - xh * HALF
        row = (((side * PHASES + (spot >> 1)) * QA + dq) * 2 + (spot & 1)) * ROWS + t
        codes.append((weigh, jnp.where((t >= 0) & (t < HALF), row, -1)))

    blocks = data.shape[0]
    load.wait()

    def widen(b, _):
        rows = pl.ds(pl.multiple_of(b * 16, 16), 16)
        rows32[rows] = slab[:, pl.ds(pl.multiple_of(b * BLK, BLK), BLK)].astype(F32)
        return 0

    lax.fori_loop(0, blocks, widen, 0, unroll=16)
    first = PART * lax.rem(group, 2)
    for c in range(PART):
        data[:, c * BLK:(c + 1) * BLK] = rows32[pl.ds(first + c, blocks, stride=16), :].astype(BF16)
    data[:, PART * BLK:] = jnp.ones((blocks, BLK), BF16)

    def sums_of(side, p):
        at = lax.broadcasted_iota(jnp.int32, (PIECE, blocks), 0) + (side * PHASES + p) * PIECE
        spread = jnp.zeros((PIECE, blocks), F32)
        for weigh, code in codes:
            spread = jnp.where(at == code, weigh, spread)
        full = jnp.dot(spread.astype(BF16), data[...], preferred_element_type=F32)
        cut = [full[:, i * BLK:(i + 1) * BLK] for i in range(PART + 1)]
        return [
            cut[i] + pltpu.roll(cut[i + 1], HALF, 0) + pltpu.roll(cut[i + 2], 2 * HALF, 0)
            for i in range(0, PART + 1, 3)
        ]

    for p in range(PHASES):
        for c, value in enumerate(sums_of(1, p)):
            part[p, :, c * BLK:(c + 1) * BLK] = value.astype(BF16)

    def remote(src, dst, ss, rs, peer):
        return pltpu.make_async_remote_copy(
            src_ref=src, dst_ref=dst, send_sem=ss, recv_sem=rs, device_id=peer, device_id_type=MESH
        )

    pl.semaphore_wait(barrier, len(peers))
    x_copies = {}
    for p in range(PHASES):
        x_copies[p] = remote(part.at[p], xin.at[p], xs.at[p], xr.at[p], x_peer)
        x_copies[p].start()
    for i, d in ((0, 7), (1, 1), (2, 6)):
        pl.semaphore_signal(relay.at[i], inc=1, device_id=b_peer[d], device_id_type=MESH)
    for copy in own[2:]:
        copy.wait()
    wy_copies = []
    for d in range(1, NY):
        ref = w_all.at[place]
        wy_copies.append(remote(ref, ref, wys.at[d], wyr.at[d], at_hid(xh, lax.rem(y + d, NY), core)))
        wy_copies[-1].start()

    quarter = PIECE // QA
    a_copies = {}
    for p in range(PHASES):
        values = sums_of(0, p)
        x_copies[p].wait_recv()
        for c, value in enumerate(values):
            lanes = slice(c * BLK, (c + 1) * BLK)
            mine[p, :, lanes] = (value + xin[p, :, lanes].astype(F32)).astype(BF16)
        for d in (2, 3, 1):
            at = pl.ds(d * quarter, quarter)
            a_copies[d, p] = remote(mine.at[p, at], ain.at[p, at], as_.at[d, p], ar.at[d, p], a_peer[d])
            a_copies[d, p].start()

    b_copies = {}

    def phase(p):
        total = mine[p, 0:quarter].astype(F32)
        for d in range(1, QA):
            a_copies[d, p].wait_recv()
        for d in range(1, QA):
            total = total + ain[p, d * quarter:(d + 1) * quarter].astype(F32)
        summed[p * quarter:(p + 1) * quarter] = total.astype(BF16)
        for spot in range(2 * p, 2 * p + 2):
            d = SPOTS[spot]
            if d:
                if d not in NEAR:
                    pl.semaphore_wait(relay.at[(3, 5, 4).index(d)], 1)
                rows = pl.ds(spot * ROWS, ROWS)
                b_copies[d] = remote(summed.at[rows], bin_.at[d], bs.at[d], br.at[d], b_peer[d])
                b_copies[d].start()

    phase(0)
    for copy in wy_copies:
        copy.wait_recv()
    ref = w_all.at[pl.ds(core * (2 * NY) + xh * NY, NY)]
    wx_copy = remote(ref, ref, wxs.at[0], wxr.at[0], at_hid(1 - xh, y, core))
    wx_copy.start()
    for p in range(1, PHASES):
        phase(p)

    r = lax.broadcasted_iota(jnp.int32, (share, BLK), 0)
    lane = lax.broadcasted_iota(jnp.int32, (share, BLK), 1)
    spare = jnp.zeros((share, BLK - share), F32)
    row = jnp.concatenate([jnp.broadcast_to(bias[...], (share, share)), spare], axis=1)
    rest = jnp.sum(jnp.where(r == lane, row, 0.0), axis=1, keepdims=True)
    channels = NG * PART
    we_wide = jnp.concatenate([we_own[...].astype(F32), jnp.zeros((share, BLK - channels), F32)], axis=1)
    for i in range(3):
        digit = rest.astype(BF16).astype(F32)
        we_wide = jnp.where(lane == channels + i, digit, we_wide)
        rest = rest - digit
    we_all[h] = we_wide.astype(BF16)

    small = []
    for d in range(1, NH):
        to = h_index[d]
        lanes = pl.ds(pl.multiple_of(tile_of(to) * BLK, BLK), BLK)
        small.append((
            remote(latent.at[:, lanes], lat_all.at[h], ls.at[d], lr.at[d], h_peer[d]),
            remote(we_all.at[h], we_all.at[h], es.at[d], er.at[d], h_peer[d]),
        ))

        @pl.when(active(to))
        def _():
            for copy in small[d - 1]:
                copy.start()

    my_lanes = pl.ds(pl.multiple_of(tile_of(h) * BLK, BLK), BLK)
    wx_copy.wait_recv()
    ref = w_all.at[pl.ds(core * (2 * NY), 2 * NY)]
    wc_copy = remote(ref, ref, wxs.at[1], wxr.at[1], at_hid(xh, y, 1 - core))
    wc_copy.start()
    gain_t[...] = jnp.broadcast_to(gain[...], (BLK, gain.shape[1])).T

    @pl.when(active(h))
    def _():
        copy = pltpu.make_async_copy(latent.at[:, my_lanes], lat_all.at[h], load_sem)
        copy.start()
        copy.wait()
        for copies in small:
            for copy in copies:
                copy.wait_recv()

    wide = w_gate.shape[1]
    wc_copy.wait_recv()
    down_t[...] = w_all[:, 2].reshape(NH * share, wide).T
    total = summed[pl.ds((KB - 1) * ROWS, ROWS)].astype(F32)
    for d in SPOTS[:-1]:
        b_copies[d].wait_recv()
        total = total + bin_[d].astype(F32)
    tiles_out[...] = jnp.zeros(tiles_out.shape, F32)
    for i in range(HALF):
        for c in range(PART + 1):
            r = HALF * (c % 3) + i
            tiles_out[i, c:c + 1] = total[r:r + 1, (c // 3) * BLK:(c // 3 + 1) * BLK]
    t_copies = []
    t_index = [xh * NG + lax.rem(group + d, NG) for d in range(NG)]
    for d in range(1, NG):
        to = t_index[d]
        src = tiles_out.at[tile_of(to) - xh * HALF]
        t_copies.append(remote(src, tiles_in.at[group], ts.at[d], tr.at[d], (lon, to)))

        @pl.when(active(to))
        def _():
            t_copies[d - 1].start()

    o_copies = []
    for d in range(1, NH):
        to = h_index[d]
        src = out_all.at[pl.ds(pl.multiple_of(to * share, share), share)]
        o_copies.append(remote(src, out.at[:, my_lanes], os_.at[d], or_.at[d], h_peer[d]))

    @pl.when(active(h))
    def _():
        tiles_in[group] = tiles_out[tile_of(h) - xh * HALF]
        for copy in t_copies:
            copy.wait_recv()
        sums = tiles_in[...]
        number = sums[0, PART:PART + 1]
        sums = sums[:, 0:PART].reshape(channels, BLK)
        extra = jnp.where(lax.broadcasted_iota(jnp.int32, (BLK - channels, BLK), 0) < 3, number, 0.0)
        sums = jnp.concatenate([sums, extra], axis=0)
        we = we_all[...].reshape(NH * share, BLK)
        smooth = jnp.zeros((NH * share, BLK), F32)
        for _ in range(2):
            digit = sums.astype(BF16)
            smooth = smooth + jnp.dot(we, digit, preferred_element_type=F32)
            sums = sums - digit.astype(F32)
        lat = lat_all[...].reshape(NH * share, BLK).astype(F32)
        mixed = (lat + scale * smooth).astype(BF16).astype(F32)
        mean_square = jnp.mean(mixed * mixed, axis=0, keepdims=True)
        normed = (mixed * lax.rsqrt(mean_square + 1e-05) * gain_t[...]).astype(BF16)
        gate = jnp.dot(w_all[:, 0].reshape(NH * share, wide), normed, preferred_element_type=F32)
        up = jnp.dot(w_all[:, 1].reshape(NH * share, wide), normed, preferred_element_type=F32)
        hidden = (gate / (1.0 + jnp.exp(-gate)) * up).astype(BF16)
        value = jnp.dot(down_t[...], hidden, preferred_element_type=F32)
        out_all[...] = (lat + value).astype(BF16)
        for copy in o_copies:
            copy.start()
        copy = pltpu.make_async_copy(
            out_all.at[pl.ds(pl.multiple_of(h * share, share), share)], out.at[:, my_lanes], load_sem
        )
        copy.start()
        copy.wait()

    for d in range(1, NH):

        @pl.when(active(lax.rem(h + NH - d, NH)))
        def _():
            o_copies[d - 1].wait_recv()

    sent = list(x_copies.values()) + list(a_copies.values()) + list(b_copies.values())
    for copy in sent + wy_copies + [wx_copy, wc_copy]:
        copy.wait_send()
    for d in range(1, NH):

        @pl.when(active(h_index[d]))
        def _():
            for copy in small[d - 1]:
                copy.wait_send()
    for d in range(1, NG):

        @pl.when(active(t_index[d]))
        def _():
            t_copies[d - 1].wait_send()

    @pl.when(active(h))
    def _():
        for copy in o_copies:
            copy.wait_send()


def local(observations, block_owner, block_tile, embed_weight, embed_bias, mesh_latent, norm_gain, w_gate, w_up, w_down):
    blocks = block_tile.shape[0]
    rows = observations.shape[0]
    share = embed_weight.shape[1]
    nodes = mesh_latent.shape[0]
    lat = norm_gain.shape[0]
    hbm = pl.BlockSpec(memory_space=pltpu.HBM)
    dma = pltpu.SemaphoreType.DMA
    out = pl.pallas_call(
        functools.partial(kernel, math.sqrt(TILES / blocks)),
        out_shape=jax.ShapeDtypeStruct((share, nodes), BF16),
        in_specs=[hbm] * 10,
        out_specs=hbm,
        scratch_shapes=[
            pltpu.VMEM((1, blocks), jnp.int32),
            pltpu.VMEM((1, blocks), jnp.int32),
            pltpu.VMEM((1, share), F32),
            pltpu.VMEM((1, lat), F32),
            pltpu.VMEM((share, NG * PART), BF16),
            pltpu.VMEM((16, rows), BF16),
            pltpu.VMEM((blocks * 16, BLK), F32),
            pltpu.VMEM((blocks, (PART + 1) * BLK), BF16),
            pltpu.VMEM((PHASES, PIECE, WIDE), BF16),
            pltpu.VMEM((PHASES, PIECE, WIDE), BF16),
            pltpu.VMEM((PHASES, PIECE, WIDE), BF16),
            pltpu.VMEM((PHASES, PIECE, WIDE), BF16),
            pltpu.VMEM((PIECE, WIDE), BF16),
            pltpu.VMEM((KB, ROWS, WIDE), BF16),
            pltpu.VMEM((HALF, 16, BLK), F32),
            pltpu.VMEM((NG, 16, BLK), F32),
            pltpu.VMEM((NH, 3, share, lat), BF16),
            pltpu.VMEM((lat, NH * share), BF16),
            pltpu.VMEM((NH, share, BLK), BF16),
            pltpu.VMEM((NH, share, BLK), BF16),
            pltpu.VMEM((lat, BLK), F32),
            pltpu.VMEM((lat, BLK), BF16),
            pltpu.SemaphoreType.REGULAR((3,)), dma, dma((8,)),
            dma((QA,)), dma((QA,)), dma((QA, PHASES)), dma((QA, PHASES)), dma((KB,)), dma((KB,)),
            dma((NY,)), dma((NY,)), dma((2,)), dma((2,)),
            dma((NH,)), dma((NH,)), dma((NH,)), dma((NH,)), dma((NH,)), dma((NH,)), dma((NH,)), dma((NH,)),
        ],
        compiler_params=pltpu.CompilerParams(collective_id=0, has_side_effects=True, vmem_limit_bytes=64 * 2**20),
    )(
        observations.T, block_owner.T, block_tile[None, :], embed_weight.T, embed_bias[None, :], mesh_latent.T, norm_gain[None, :],
        w_gate.T, w_up.T, w_down,
    )
    return out.T


def solution(mesh):
    return jax.shard_map(
        local,
        mesh=mesh,
        in_specs=(
            P("lon", None),
            P("lon", None),
            P("lon"),
            P(None, "hid"),
            P("hid"),
            P("lon", "hid"),
            P(),
            P(None, "hid"),
            P(None, "hid"),
            P("hid", None),
        ),
        out_specs=P("lon", "hid"),
        check_vma=False,
    )
```

```python
import functools
import math

import jax
import jax.numpy as jnp
from jax import lax
from jax.experimental import pallas as pl
from jax.experimental.pallas import tpu as pltpu
from jax.sharding import PartitionSpec as P

MESH = pl.DeviceIdType.MESH
BLK = 128
NX = 2
NZ = 32
NH = 16
NY = 4
LON = NX * NZ
QA = 4
KB = NZ // QA
TILES = 10
ROWS = 16
PART = 8
NG = NH // 2
HALF = TILES // 2
WIDE = 3 * BLK
PIECE = KB * ROWS
PHASES = KB // 2
SPOTS = (4, 3, 5, 2, 6, 1, 7, 0)
NEAR = (1, 7, 2, 6)
F32 = jnp.float32
BF16 = jnp.bfloat16


def kernel(
    scale,
    obs, owner_in, tile_in, weight, bias_in, latent, gain_in, w_gate, w_up, w_down,
    out,
    owner, tile, bias, gain, we_own, slab, rows32, data, part, xin, mine, ain, summed, bin_,
    tiles_out, tiles_in, w_all, down_t, we_all, lat_all, gain_t, out_all,
    relay, load_sem, own_sem, xs, xr, as_, ar, bs, br, wys, wyr, wxs, wxr, es, er, ls, lr, ts, tr, os_, or_,
):
    lon = lax.axis_index("lon")
    h = lax.axis_index("hid")
    group = lax.rem(h, NG)
    x = lon // NZ
    z = lax.rem(lon, NZ)
    core = lax.rem(h, 2)
    y = lax.rem(h // 2, NY)
    xh = h // (2 * NY)
    off = 2 * core
    v = lax.rem(z + off, NZ)
    g = v // QA
    q = lax.rem(v, QA)

    def at_v(value):
        return (x * NZ + lax.rem(value - off + NZ, NZ), h)

    def at_hid(xh, y, core):
        return (lon, (xh * NY + y) * 2 + core)

    def active(to):
        return (lax.rem(to, 2) == 0) | (lax.rem(to // 2, NY) == 0)

    def tile_of(to):
        return (to // (2 * NY)) * (NY + 1) + jnp.where(lax.rem(to, 2) == 0, lax.rem(to // 2, NY), NY)

    x_peer = (lax.rem(x + 1, NX) * NZ + z, h)
    a_peer = [at_v(g * QA + lax.rem(q + d, QA)) for d in range(QA)]
    b_peer = [at_v(lax.rem(g + d, KB) * QA + q) for d in range(KB)]
    h_index = [lax.rem(h + d, NH) for d in range(NH)]
    h_peer = [(lon, i) for i in h_index]

    barrier = pltpu.get_barrier_semaphore()
    peers = [x_peer] + a_peer[1:] + [b_peer[d] for d in NEAR] + h_peer[1:]
    for peer in peers:
        pl.semaphore_signal(barrier, inc=1, device_id=peer, device_id_type=MESH)

    load = pltpu.make_async_copy(obs.at[pl.ds(pl.multiple_of((group // 2) * 16, 16), 16)], slab, load_sem)
    load.start()
    share = w_down.shape[0]
    place = core * (2 * NY) + xh * NY + y
    own = [
        pltpu.make_async_copy(owner_in, owner, own_sem.at[0]),
        pltpu.make_async_copy(tile_in, tile, own_sem.at[1]),
        pltpu.make_async_copy(w_gate, w_all.at[place, 0], own_sem.at[2]),
        pltpu.make_async_copy(w_up, w_all.at[place, 1], own_sem.at[3]),
        pltpu.make_async_copy(w_down, w_all.at[place, 2], own_sem.at[4]),
        pltpu.make_async_copy(bias_in, bias, own_sem.at[5]),
        pltpu.make_async_copy(gain_in, gain, own_sem.at[6]),
        pltpu.make_async_copy(weight, we_own, own_sem.at[7]),
    ]
    for copy in own:
        copy.start()
    own[0].wait()
    own[1].wait()

    codes = []
    for step, weigh in ((0, 1.0), (-1, 0.5), (1, 0.5)):
        t = tile[...] + step
        o = owner[...]
        o = jnp.where(t < 0, (o + LON - 1) & (LON - 1), jnp.where(t >= TILES, (o + 1) & (LON - 1), o))
        t = jnp.where(t < 0, TILES - 1, jnp.where(t >= TILES, 0, t))
        u = ((o & (NZ - 1)) + off) & (NZ - 1)
        side = (o >> 5) ^ x
        dq = ((u & (QA - 1)) - q) & (QA - 1)
        dk = ((u >> 2) - g) & (KB - 1)
        spot = jnp.full(dk.shape, KB - 1, jnp.int32)
        for place_of, d in enumerate(SPOTS[:-1]):
            spot = jnp.where(dk == d, place_of, spot)
        t = t - xh * HALF
        row = (((side * PHASES + (spot >> 1)) * QA + dq) * 2 + (spot & 1)) * ROWS + t
        codes.append((weigh, jnp.where((t >= 0) & (t < HALF), row, -1)))

    blocks = data.shape[0]
    load.wait()

    def widen(b, _):
        rows = pl.ds(pl.multiple_of(b * 16, 16), 16)
        rows32[rows] = slab[:, pl.ds(pl.multiple_of(b * BLK, BLK), BLK)].astype(F32)
        return 0

    lax.fori_loop(0, blocks, widen, 0, unroll=16)
    first = PART * lax.rem(group, 2)
    for c in range(PART):
        data[:, c * BLK:(c + 1) * BLK] = rows32[pl.ds(first + c, blocks, stride=16), :].astype(BF16)
    data[:, PART * BLK:] = jnp.ones((blocks, BLK), BF16)

    def sums_of(side, p):
        at = lax.broadcasted_iota(jnp.int32, (PIECE, blocks), 0) + (side * PHASES + p) * PIECE
        spread = jnp.zeros((PIECE, blocks), F32)
        for weigh, code in codes:
            spread = jnp.where(at == code, weigh, spread)
        full = jnp.dot(spread.astype(BF16), data[...], preferred_element_type=F32)
        cut = [full[:, i * BLK:(i + 1) * BLK] for i in range(PART + 1)]
        return [
            cut[i] + pltpu.roll(cut[i + 1], HALF, 0) + pltpu.roll(cut[i + 2], 2 * HALF, 0)
            for i in range(0, PART + 1, 3)
        ]

    for p in range(PHASES):
        for c, value in enumerate(sums_of(1, p)):
            part[p, :, c * BLK:(c + 1) * BLK] = value.astype(BF16)

    def remote(src, dst, ss, rs, peer):
        return pltpu.make_async_remote_copy(
            src_ref=src, dst_ref=dst, send_sem=ss, recv_sem=rs, device_id=peer, device_id_type=MESH
        )

    pl.semaphore_wait(barrier, len(peers))
    x_copies = {}
    for p in range(PHASES):
        x_copies[p] = remote(part.at[p], xin.at[p], xs.at[p], xr.at[p], x_peer)
        x_copies[p].start()
    for i, d in ((0, 7), (1, 1), (2, 6)):
        pl.semaphore_signal(relay.at[i], inc=1, device_id=b_peer[d], device_id_type=MESH)
    for copy in own[2:]:
        copy.wait()
    wy_copies = []
    for d in range(1, NY):
        ref = w_all.at[place]
        wy_copies.append(remote(ref, ref, wys.at[d], wyr.at[d], at_hid(xh, lax.rem(y + d, NY), core)))
        wy_copies[-1].start()

    quarter = PIECE // QA
    a_copies = {}
    for p in range(PHASES):
        values = sums_of(0, p)
        x_copies[p].wait_recv()
        for c, value in enumerate(values):
            lanes = slice(c * BLK, (c + 1) * BLK)
            mine[p, :, lanes] = (value + xin[p, :, lanes].astype(F32)).astype(BF16)
        for d in (2, 3, 1):
            at = pl.ds(d * quarter, quarter)
            a_copies[d, p] = remote(mine.at[p, at], ain.at[p, at], as_.at[d, p], ar.at[d, p], a_peer[d])
            a_copies[d, p].start()

    b_copies = {}

    def phase(p):
        total = mine[p, 0:quarter].astype(F32)
        for d in range(1, QA):
            a_copies[d, p].wait_recv()
        for d in range(1, QA):
            total = total + ain[p, d * quarter:(d + 1) * quarter].astype(F32)
        summed[p * quarter:(p + 1) * quarter] = total.astype(BF16)
        for spot in range(2 * p, 2 * p + 2):
            d = SPOTS[spot]
            if d:
                if d not in NEAR:
                    pl.semaphore_wait(relay.at[(3, 5, 4).index(d)], 1)
                rows = pl.ds(spot * ROWS, ROWS)
                b_copies[d] = remote(summed.at[rows], bin_.at[d], bs.at[d], br.at[d], b_peer[d])
                b_copies[d].start()

    phase(0)
    for copy in wy_copies:
        copy.wait_recv()
    ref = w_all.at[pl.ds(core * (2 * NY) + xh * NY, NY)]
    wx_copy = remote(ref, ref, wxs.at[0], wxr.at[0], at_hid(1 - xh, y, core))
    wx_copy.start()
    for p in range(1, PHASES):
        phase(p)

    r = lax.broadcasted_iota(jnp.int32, (share, BLK), 0)
    lane = lax.broadcasted_iota(jnp.int32, (share, BLK), 1)
    spare = jnp.zeros((share, BLK - share), F32)
    row = jnp.concatenate([jnp.broadcast_to(bias[...], (share, share)), spare], axis=1)
    rest = jnp.sum(jnp.where(r == lane, row, 0.0), axis=1, keepdims=True)
    channels = NG * PART
    we_wide = jnp.concatenate([we_own[...].astype(F32), jnp.zeros((share, BLK - channels), F32)], axis=1)
    for i in range(3):
        digit = rest.astype(BF16).astype(F32)
        we_wide = jnp.where(lane == channels + i, digit, we_wide)
        rest = rest - digit
    we_all[h] = we_wide.astype(BF16)

    small = []
    for d in range(1, NH):
        to = h_index[d]
        lanes = pl.ds(pl.multiple_of(tile_of(to) * BLK, BLK), BLK)
        small.append((
            remote(latent.at[:, lanes], lat_all.at[h], ls.at[d], lr.at[d], h_peer[d]),
            remote(we_all.at[h], we_all.at[h], es.at[d], er.at[d], h_peer[d]),
        ))

        @pl.when(active(to))
        def _():
            for copy in small[d - 1]:
                copy.start()

    my_lanes = pl.ds(pl.multiple_of(tile_of(h) * BLK, BLK), BLK)
    wx_copy.wait_recv()
    ref = w_all.at[pl.ds(core * (2 * NY), 2 * NY)]
    wc_copy = remote(ref, ref, wxs.at[1], wxr.at[1], at_hid(xh, y, 1 - core))
    wc_copy.start()
    gain_t[...] = jnp.broadcast_to(gain[...], (BLK, gain.shape[1])).T

    @pl.when(active(h))
    def _():
        copy = pltpu.make_async_copy(latent.at[:, my_lanes], lat_all.at[h], load_sem)
        copy.start()
        copy.wait()
        for copies in small:
            for copy in copies:
                copy.wait_recv()

    wide = w_gate.shape[1]
    wc_copy.wait_recv()
    down_t[...] = w_all[:, 2].reshape(NH * share, wide).T
    total = summed[pl.ds((KB - 1) * ROWS, ROWS)].astype(F32)
    for d in SPOTS[:-1]:
        b_copies[d].wait_recv()
        total = total + bin_[d].astype(F32)
    tiles_out[...] = jnp.zeros(tiles_out.shape, F32)
    for i in range(HALF):
        for c in range(PART + 1):
            r = HALF * (c % 3) + i
            tiles_out[i, c:c + 1] = total[r:r + 1, (c // 3) * BLK:(c // 3 + 1) * BLK]
    t_copies = []
    t_index = [xh * NG + lax.rem(group + d, NG) for d in range(NG)]
    for d in range(1, NG):
        to = t_index[d]
        src = tiles_out.at[tile_of(to) - xh * HALF]
        t_copies.append(remote(src, tiles_in.at[group], ts.at[d], tr.at[d], (lon, to)))

        @pl.when(active(to))
        def _():
            t_copies[d - 1].start()

    o_copies = []
    for d in range(1, NH):
        to = h_index[d]
        src = out_all.at[pl.ds(pl.multiple_of(to * share, share), share)]
        o_copies.append(remote(src, out.at[:, my_lanes], os_.at[d], or_.at[d], h_peer[d]))

    @pl.when(active(h))
    def _():
        tiles_in[group] = tiles_out[tile_of(h) - xh * HALF]
        for copy in t_copies:
            copy.wait_recv()
        sums = tiles_in[...]
        number = sums[0, PART:PART + 1]
        sums = sums[:, 0:PART].reshape(channels, BLK)
        extra = jnp.where(lax.broadcasted_iota(jnp.int32, (BLK - channels, BLK), 0) < 3, number, 0.0)
        sums = jnp.concatenate([sums, extra], axis=0)
        we = we_all[...].reshape(NH * share, BLK)
        smooth = jnp.zeros((NH * share, BLK), F32)
        for _ in range(2):
            digit = sums.astype(BF16)
            smooth = smooth + jnp.dot(we, digit, preferred_element_type=F32)
            sums = sums - digit.astype(F32)
        lat = lat_all[...].reshape(NH * share, BLK).astype(F32)
        mixed = (lat + scale * smooth).astype(BF16).astype(F32)
        mean_square = jnp.mean(mixed * mixed, axis=0, keepdims=True)
        normed = (mixed * lax.rsqrt(mean_square + 1e-05) * gain_t[...]).astype(BF16)
        gate = jnp.dot(w_all[:, 0].reshape(NH * share, wide), normed, preferred_element_type=F32)
        up = jnp.dot(w_all[:, 1].reshape(NH * share, wide), normed, preferred_element_type=F32)
        hidden = (gate / (1.0 + jnp.exp(-gate)) * up).astype(BF16)
        value = jnp.dot(down_t[...], hidden, preferred_element_type=F32)
        out_all[...] = (lat + value).astype(BF16)
        for copy in o_copies:
            copy.start()
        copy = pltpu.make_async_copy(
            out_all.at[pl.ds(pl.multiple_of(h * share, share), share)], out.at[:, my_lanes], load_sem
        )
        copy.start()
        copy.wait()

    for d in range(1, NH):

        @pl.when(active(lax.rem(h + NH - d, NH)))
        def _():
            o_copies[d - 1].wait_recv()

    sent = list(x_copies.values()) + list(a_copies.values()) + list(b_copies.values())
    for copy in sent + wy_copies + [wx_copy, wc_copy]:
        copy.wait_send()
    for d in range(1, NH):

        @pl.when(active(h_index[d]))
        def _():
            for copy in small[d - 1]:
                copy.wait_send()
    for d in range(1, NG):

        @pl.when(active(t_index[d]))
        def _():
            t_copies[d - 1].wait_send()

    @pl.when(active(h))
    def _():
        for copy in o_copies:
            copy.wait_send()


def local(observations, block_owner, block_tile, embed_weight, embed_bias, mesh_latent, norm_gain, w_gate, w_up, w_down):
    blocks = block_tile.shape[0]
    rows = observations.shape[0]
    share = embed_weight.shape[1]
    nodes = mesh_latent.shape[0]
    lat = norm_gain.shape[0]
    hbm = pl.BlockSpec(memory_space=pltpu.HBM)
    dma = pltpu.SemaphoreType.DMA
    out = pl.pallas_call(
        functools.partial(kernel, math.sqrt(TILES / blocks)),
        out_shape=jax.ShapeDtypeStruct((share, nodes), BF16),
        in_specs=[hbm] * 10,
        out_specs=hbm,
        scratch_shapes=[
            pltpu.VMEM((1, blocks), jnp.int32),
            pltpu.VMEM((1, blocks), jnp.int32),
            pltpu.VMEM((1, share), F32),
            pltpu.VMEM((1, lat), F32),
            pltpu.VMEM((share, NG * PART), BF16),
            pltpu.VMEM((16, rows), BF16),
            pltpu.VMEM((blocks * 16, BLK), F32),
            pltpu.VMEM((blocks, (PART + 1) * BLK), BF16),
            pltpu.VMEM((PHASES, PIECE, WIDE), BF16),
            pltpu.VMEM((PHASES, PIECE, WIDE), BF16),
            pltpu.VMEM((PHASES, PIECE, WIDE), BF16),
            pltpu.VMEM((PHASES, PIECE, WIDE), BF16),
            pltpu.VMEM((PIECE, WIDE), BF16),
            pltpu.VMEM((KB, ROWS, WIDE), BF16),
            pltpu.VMEM((HALF, 16, BLK), F32),
            pltpu.VMEM((NG, 16, BLK), F32),
            pltpu.VMEM((NH, 3, share, lat), BF16),
            pltpu.VMEM((lat, NH * share), BF16),
            pltpu.VMEM((NH, share, BLK), BF16),
            pltpu.VMEM((NH, share, BLK), BF16),
            pltpu.VMEM((lat, BLK), F32),
            pltpu.VMEM((lat, BLK), BF16),
            pltpu.SemaphoreType.REGULAR((3,)), dma, dma((8,)),
            dma((QA,)), dma((QA,)), dma((QA, PHASES)), dma((QA, PHASES)), dma((KB,)), dma((KB,)),
            dma((NY,)), dma((NY,)), dma((2,)), dma((2,)),
            dma((NH,)), dma((NH,)), dma((NH,)), dma((NH,)), dma((NH,)), dma((NH,)), dma((NH,)), dma((NH,)),
        ],
        compiler_params=pltpu.CompilerParams(collective_id=0, has_side_effects=True, vmem_limit_bytes=64 * 2**20),
    )(
        observations.T, block_owner.T, block_tile[None, :], embed_weight.T, embed_bias[None, :], mesh_latent.T, norm_gain[None, :],
        w_gate.T, w_up.T, w_down,
    )
    return out.T


def solution(mesh):
    return jax.shard_map(
        local,
        mesh=mesh,
        in_specs=(
            P("lon", None),
            P("lon", None),
            P("lon"),
            P(None, "hid"),
            P("hid"),
            P("lon", "hid"),
            P(),
            P(None, "hid"),
            P(None, "hid"),
            P("hid", None),
        ),
        out_specs=P("lon", "hid"),
        check_vma=False,
    )
```

```python
import functools
import math

import jax
import jax.numpy as jnp
from jax import lax
from jax.experimental import pallas as pl
from jax.experimental.pallas import tpu as pltpu
from jax.sharding import PartitionSpec as P

MESH = pl.DeviceIdType.MESH
BLK = 128
NX = 2
NZ = 32
NH = 16
NY = 4
LON = NX * NZ
QA = 4
KB = NZ // QA
TILES = 10
ROWS = 16
PART = 8
NG = NH // 2
HALF = TILES // 2
WIDE = 3 * BLK
PIECE = KB * ROWS
PHASES = KB // 2
SPOTS = (4, 3, 5, 2, 6, 1, 7, 0)
NEAR = (1, 7, 2, 6)
F32 = jnp.float32
BF16 = jnp.bfloat16


def kernel(
    scale,
    obs, owner_in, tile_in, weight, bias_in, latent, gain_in, w_gate, w_up, w_down,
    out,
    owner, tile, bias, gain, we_own, slab, rows32, data, part, xin, mine, ain, summed, bin_,
    tiles_out, tiles_in, w_all, down_t, we_all, lat_all, gain_t, out_all,
    relay, load_sem, own_sem, xs, xr, as_, ar, bs, br, wys, wyr, wxs, wxr, es, er, ls, lr, ts, tr, os_, or_,
):
    lon = lax.axis_index("lon")
    h = lax.axis_index("hid")
    group = lax.rem(h, NG)
    x = lon // NZ
    z = lax.rem(lon, NZ)
    core = lax.rem(h, 2)
    y = lax.rem(h // 2, NY)
    xh = h // (2 * NY)
    g = z // QA
    q = lax.rem(z, QA)

    def at_v(value):
        return (x * NZ + value, h)

    def at_hid(xh, y, core):
        return (lon, (xh * NY + y) * 2 + core)

    def active(to):
        return (lax.rem(to, 2) == 0) | (lax.rem(to // 2, NY) == 0)

    def tile_of(to):
        return (to // (2 * NY)) * (NY + 1) + jnp.where(lax.rem(to, 2) == 0, lax.rem(to // 2, NY), NY)

    x_peer = (lax.rem(x + 1, NX) * NZ + z, h)
    a_peer = [at_v(g * QA + lax.rem(q + d, QA)) for d in range(QA)]
    b_peer = [at_v(lax.rem(g + d, KB) * QA + q) for d in range(KB)]
    h_index = [lax.rem(h + d, NH) for d in range(NH)]
    h_peer = [(lon, i) for i in h_index]

    barrier = pltpu.get_barrier_semaphore()
    peers = [x_peer] + a_peer[1:] + [b_peer[d] for d in NEAR] + h_peer[1:]
    for peer in peers:
        pl.semaphore_signal(barrier, inc=1, device_id=peer, device_id_type=MESH)

    load = pltpu.make_async_copy(obs.at[pl.ds(pl.multiple_of((group // 2) * 16, 16), 16)], slab, load_sem)
    load.start()
    share = w_down.shape[0]
    place = core * (2 * NY) + xh * NY + y
    own = [
        pltpu.make_async_copy(owner_in, owner, own_sem.at[0]),
        pltpu.make_async_copy(tile_in, tile, own_sem.at[1]),
        pltpu.make_async_copy(w_gate, w_all.at[place, 0], own_sem.at[2]),
        pltpu.make_async_copy(w_up, w_all.at[place, 1], own_sem.at[3]),
        pltpu.make_async_copy(w_down, w_all.at[place, 2], own_sem.at[4]),
        pltpu.make_async_copy(bias_in, bias, own_sem.at[5]),
        pltpu.make_async_copy(gain_in, gain, own_sem.at[6]),
        pltpu.make_async_copy(weight, we_own, own_sem.at[7]),
    ]
    for copy in own:
        copy.start()
    own[0].wait()
    own[1].wait()

    codes = []
    for step, weigh in ((0, 1.0), (-1, 0.5), (1, 0.5)):
        t = tile[...] + step
        o = owner[...]
        o = jnp.where(t < 0, (o + LON - 1) & (LON - 1), jnp.where(t >= TILES, (o + 1) & (LON - 1), o))
        t = jnp.where(t < 0, TILES - 1, jnp.where(t >= TILES, 0, t))
        u = o & (NZ - 1)
        side = (o >> 5) ^ x
        dq = ((u & (QA - 1)) - q) & (QA - 1)
        dk = ((u >> 2) - g) & (KB - 1)
        spot = jnp.full(dk.shape, KB - 1, jnp.int32)
        for place_of, d in enumerate(SPOTS[:-1]):
            spot = jnp.where(dk == d, place_of, spot)
        t = t - xh * HALF
        row = (((side * PHASES + (spot >> 1)) * QA + dq) * 2 + (spot & 1)) * ROWS + t
        codes.append((weigh, jnp.where((t >= 0) & (t < HALF), row, -1)))

    blocks = data.shape[0]
    load.wait()

    def widen(b, _):
        rows = pl.ds(pl.multiple_of(b * 16, 16), 16)
        rows32[rows] = slab[:, pl.ds(pl.multiple_of(b * BLK, BLK), BLK)].astype(F32)
        return 0

    lax.fori_loop(0, blocks, widen, 0, unroll=16)
    first = PART * lax.rem(group, 2)
    for c in range(PART):
        data[:, c * BLK:(c + 1) * BLK] = rows32[pl.ds(first + c, blocks, stride=16), :].astype(BF16)
    data[:, PART * BLK:] = jnp.ones((blocks, BLK), BF16)

    def sums_of(side, p):
        at = lax.broadcasted_iota(jnp.int32, (PIECE, blocks), 0) + (side * PHASES + p) * PIECE
        spread = jnp.zeros((PIECE, blocks), F32)
        for weigh, code in codes:
            spread = jnp.where(at == code, weigh, spread)
        full = jnp.dot(spread.astype(BF16), data[...], preferred_element_type=F32)
        cut = [full[:, i * BLK:(i + 1) * BLK] for i in range(PART + 1)]
        return [
            cut[i] + pltpu.roll(cut[i + 1], HALF, 0) + pltpu.roll(cut[i + 2], 2 * HALF, 0)
            for i in range(0, PART + 1, 3)
        ]

    for p in range(PHASES):
        for c, value in enumerate(sums_of(1, p)):
            part[p, :, c * BLK:(c + 1) * BLK] = value.astype(BF16)

    def remote(src, dst, ss, rs, peer):
        return pltpu.make_async_remote_copy(
            src_ref=src, dst_ref=dst, send_sem=ss, recv_sem=rs, device_id=peer, device_id_type=MESH
        )

    pl.semaphore_wait(barrier, len(peers))
    x_copies = {}
    for p in range(PHASES):
        x_copies[p] = remote(part.at[p], xin.at[p], xs.at[p], xr.at[p], x_peer)
        x_copies[p].start()
    for i, d in ((0, 7), (1, 1), (2, 6)):
        pl.semaphore_signal(relay.at[i], inc=1, device_id=b_peer[d], device_id_type=MESH)
    for copy in own[2:]:
        copy.wait()
    wy_copies = []
    for d in range(1, NY):
        ref = w_all.at[place]
        wy_copies.append(remote(ref, ref, wys.at[d], wyr.at[d], at_hid(xh, lax.rem(y + d, NY), core)))
        wy_copies[-1].start()

    quarter = PIECE // QA
    a_copies = {}
    for p in range(PHASES):
        values = sums_of(0, p)
        x_copies[p].wait_recv()
        for c, value in enumerate(values):
            lanes = slice(c * BLK, (c + 1) * BLK)
            mine[p, :, lanes] = (value + xin[p, :, lanes].astype(F32)).astype(BF16)
        for d in (2, 3, 1):
            at = pl.ds(d * quarter, quarter)
            a_copies[d, p] = remote(mine.at[p, at], ain.at[p, at], as_.at[d, p], ar.at[d, p], a_peer[d])
            a_copies[d, p].start()

    b_copies = {}

    def phase(p):
        total = mine[p, 0:quarter].astype(F32)
        for d in range(1, QA):
            a_copies[d, p].wait_recv()
        for d in range(1, QA):
            total = total + ain[p, d * quarter:(d + 1) * quarter].astype(F32)
        summed[p * quarter:(p + 1) * quarter] = total.astype(BF16)
        for spot in range(2 * p, 2 * p + 2):
            d = SPOTS[spot]
            if d:
                if d not in NEAR:
                    pl.semaphore_wait(relay.at[(3, 5, 4).index(d)], 1)
                rows = pl.ds(spot * ROWS, ROWS)
                b_copies[d] = remote(summed.at[rows], bin_.at[d], bs.at[d], br.at[d], b_peer[d])
                b_copies[d].start()

    phase(0)
    for copy in wy_copies:
        copy.wait_recv()
    ref = w_all.at[pl.ds(core * (2 * NY) + xh * NY, NY)]
    wx_copy = remote(ref, ref, wxs.at[0], wxr.at[0], at_hid(1 - xh, y, core))
    wx_copy.start()
    for p in range(1, PHASES):
        phase(p)

    r = lax.broadcasted_iota(jnp.int32, (share, BLK), 0)
    lane = lax.broadcasted_iota(jnp.int32, (share, BLK), 1)
    spare = jnp.zeros((share, BLK - share), F32)
    row = jnp.concatenate([jnp.broadcast_to(bias[...], (share, share)), spare], axis=1)
    rest = jnp.sum(jnp.where(r == lane, row, 0.0), axis=1, keepdims=True)
    channels = NG * PART
    we_wide = jnp.concatenate([we_own[...].astype(F32), jnp.zeros((share, BLK - channels), F32)], axis=1)
    for i in range(3):
        digit = rest.astype(BF16).astype(F32)
        we_wide = jnp.where(lane == channels + i, digit, we_wide)
        rest = rest - digit
    we_all[h] = we_wide.astype(BF16)

    small = []
    for d in range(1, NH):
        to = h_index[d]
        lanes = pl.ds(pl.multiple_of(tile_of(to) * BLK, BLK), BLK)
        small.append((
            remote(latent.at[:, lanes], lat_all.at[h], ls.at[d], lr.at[d], h_peer[d]),
            remote(we_all.at[h], we_all.at[h], es.at[d], er.at[d], h_peer[d]),
        ))

        @pl.when(active(to))
        def _():
            for copy in small[d - 1]:
                copy.start()

    my_lanes = pl.ds(pl.multiple_of(tile_of(h) * BLK, BLK), BLK)
    wx_copy.wait_recv()
    ref = w_all.at[pl.ds(core * (2 * NY), 2 * NY)]
    wc_copy = remote(ref, ref, wxs.at[1], wxr.at[1], at_hid(xh, y, 1 - core))
    wc_copy.start()
    gain_t[...] = jnp.broadcast_to(gain[...], (BLK, gain.shape[1])).T

    @pl.when(active(h))
    def _():
        copy = pltpu.make_async_copy(latent.at[:, my_lanes], lat_all.at[h], load_sem)
        copy.start()
        copy.wait()
        for copies in small:
            for copy in copies:
                copy.wait_recv()

    wide = w_gate.shape[1]
    wc_copy.wait_recv()
    down_t[...] = w_all[:, 2].reshape(NH * share, wide).T
    total = summed[pl.ds((KB - 1) * ROWS, ROWS)].astype(F32)
    for d in SPOTS[:-1]:
        b_copies[d].wait_recv()
        total = total + bin_[d].astype(F32)
    tiles_out[...] = jnp.zeros(tiles_out.shape, F32)
    for i in range(HALF):
        for c in range(PART + 1):
            r = HALF * (c % 3) + i
            tiles_out[i, c:c + 1] = total[r:r + 1, (c // 3) * BLK:(c // 3 + 1) * BLK]
    t_copies = []
    t_index = [xh * NG + lax.rem(group + d, NG) for d in range(NG)]
    for d in range(1, NG):
        to = t_index[d]
        src = tiles_out.at[tile_of(to) - xh * HALF]
        t_copies.append(remote(src, tiles_in.at[group], ts.at[d], tr.at[d], (lon, to)))

        @pl.when(active(to))
        def _():
            t_copies[d - 1].start()

    o_copies = []
    for d in range(1, NH):
        to = h_index[d]
        src = out_all.at[pl.ds(pl.multiple_of(to * share, share), share)]
        o_copies.append(remote(src, out.at[:, my_lanes], os_.at[d], or_.at[d], h_peer[d]))

    @pl.when(active(h))
    def _():
        tiles_in[group] = tiles_out[tile_of(h) - xh * HALF]
        for copy in t_copies:
            copy.wait_recv()
        sums = tiles_in[...]
        number = sums[0, PART:PART + 1]
        sums = sums[:, 0:PART].reshape(channels, BLK)
        extra = jnp.where(lax.broadcasted_iota(jnp.int32, (BLK - channels, BLK), 0) < 3, number, 0.0)
        sums = jnp.concatenate([sums, extra], axis=0)
        we = we_all[...].reshape(NH * share, BLK)
        smooth = jnp.zeros((NH * share, BLK), F32)
        for _ in range(2):
            digit = sums.astype(BF16)
            smooth = smooth + jnp.dot(we, digit, preferred_element_type=F32)
            sums = sums - digit.astype(F32)
        lat = lat_all[...].reshape(NH * share, BLK).astype(F32)
        mixed = (lat + scale * smooth).astype(BF16).astype(F32)
        mean_square = jnp.mean(mixed * mixed, axis=0, keepdims=True)
        normed = (mixed * lax.rsqrt(mean_square + 1e-05) * gain_t[...]).astype(BF16)
        gate = jnp.dot(w_all[:, 0].reshape(NH * share, wide), normed, preferred_element_type=F32)
        up = jnp.dot(w_all[:, 1].reshape(NH * share, wide), normed, preferred_element_type=F32)
        hidden = (gate / (1.0 + jnp.exp(-gate)) * up).astype(BF16)
        value = jnp.dot(down_t[...], hidden, preferred_element_type=F32)
        out_all[...] = (lat + value).astype(BF16)
        for copy in o_copies:
            copy.start()
        copy = pltpu.make_async_copy(
            out_all.at[pl.ds(pl.multiple_of(h * share, share), share)], out.at[:, my_lanes], load_sem
        )
        copy.start()
        copy.wait()

    for d in range(1, NH):

        @pl.when(active(lax.rem(h + NH - d, NH)))
        def _():
            o_copies[d - 1].wait_recv()

    sent = list(x_copies.values()) + list(a_copies.values()) + list(b_copies.values())
    for copy in sent + wy_copies + [wx_copy, wc_copy]:
        copy.wait_send()
    for d in range(1, NH):

        @pl.when(active(h_index[d]))
        def _():
            for copy in small[d - 1]:
                copy.wait_send()
    for d in range(1, NG):

        @pl.when(active(t_index[d]))
        def _():
            t_copies[d - 1].wait_send()

    @pl.when(active(h))
    def _():
        for copy in o_copies:
            copy.wait_send()


def local(observations, block_owner, block_tile, embed_weight, embed_bias, mesh_latent, norm_gain, w_gate, w_up, w_down):
    blocks = block_tile.shape[0]
    rows = observations.shape[0]
    share = embed_weight.shape[1]
    nodes = mesh_latent.shape[0]
    lat = norm_gain.shape[0]
    hbm = pl.BlockSpec(memory_space=pltpu.HBM)
    dma = pltpu.SemaphoreType.DMA
    out = pl.pallas_call(
        functools.partial(kernel, math.sqrt(TILES / blocks)),
        out_shape=jax.ShapeDtypeStruct((share, nodes), BF16),
        in_specs=[hbm] * 10,
        out_specs=hbm,
        scratch_shapes=[
            pltpu.VMEM((1, blocks), jnp.int32),
            pltpu.VMEM((1, blocks), jnp.int32),
            pltpu.VMEM((1, share), F32),
            pltpu.VMEM((1, lat), F32),
            pltpu.VMEM((share, NG * PART), BF16),
            pltpu.VMEM((16, rows), BF16),
            pltpu.VMEM((blocks * 16, BLK), F32),
            pltpu.VMEM((blocks, (PART + 1) * BLK), BF16),
            pltpu.VMEM((PHASES, PIECE, WIDE), BF16),
            pltpu.VMEM((PHASES, PIECE, WIDE), BF16),
            pltpu.VMEM((PHASES, PIECE, WIDE), BF16),
            pltpu.VMEM((PHASES, PIECE, WIDE), BF16),
            pltpu.VMEM((PIECE, WIDE), BF16),
            pltpu.VMEM((KB, ROWS, WIDE), BF16),
            pltpu.VMEM((HALF, 16, BLK), F32),
            pltpu.VMEM((NG, 16, BLK), F32),
            pltpu.VMEM((NH, 3, share, lat), BF16),
            pltpu.VMEM((lat, NH * share), BF16),
            pltpu.VMEM((NH, share, BLK), BF16),
            pltpu.VMEM((NH, share, BLK), BF16),
            pltpu.VMEM((lat, BLK), F32),
            pltpu.VMEM((lat, BLK), BF16),
            pltpu.SemaphoreType.REGULAR((3,)), dma, dma((8,)),
            dma((QA,)), dma((QA,)), dma((QA, PHASES)), dma((QA, PHASES)), dma((KB,)), dma((KB,)),
            dma((NY,)), dma((NY,)), dma((2,)), dma((2,)),
            dma((NH,)), dma((NH,)), dma((NH,)), dma((NH,)), dma((NH,)), dma((NH,)), dma((NH,)), dma((NH,)),
        ],
        compiler_params=pltpu.CompilerParams(collective_id=0, has_side_effects=True, vmem_limit_bytes=64 * 2**20),
    )(
        observations.T, block_owner.T, block_tile[None, :], embed_weight.T, embed_bias[None, :], mesh_latent.T, norm_gain[None, :],
        w_gate.T, w_up.T, w_down,
    )
    return out.T


def solution(mesh):
    return jax.shard_map(
        local,
        mesh=mesh,
        in_specs=(
            P("lon", None),
            P("lon", None),
            P("lon"),
            P(None, "hid"),
            P("hid"),
            P("lon", "hid"),
            P(),
            P(None, "hid"),
            P(None, "hid"),
            P("hid", None),
        ),
        out_specs=P("lon", "hid"),
        check_vma=False,
    )
```
